512 devices in a mesh: dp: 32 (over x, y, core), tensor: 16 (over z).
Axes of the slice: x: 4, y: 4, z: 16, core: 2. Of those that a mesh axis runs over, the one named last changes fastest.
Arguments:
- tokens: bfloat16 [2048, 14848], P('dp', 'tensor'), may hold values from -6 to 6
- base_up_matrix: bfloat16 [14848, 32, 928], P('tensor', 'dp'), may hold values from -0.046875 to 0.046875
- adapter_down_maps: bfloat16 [64, 64, 14848], P('dp', None, 'tensor'), may hold values from -0.046875 to 0.046875
- adapter_up_maps: bfloat16 [64, 64, 29696], P('dp', None, 'tensor'), may hold values from -0.75 to 0.75
- request_adapter: int32 [2048, 1], P('dp'), may hold values from 0 to 63; in each aligned block of 64 rows (0 to 63, 64 to 127, ...) at most 2 rows name the same one
- adapter_storage: int32 [64], replicated, may hold values from 0 to 63, each once
Outputs:
- hidden: bfloat16 [2048, 29696], P('dp', 'tensor')
The draws below stay inside these ranges and needn't reach their ends.
Inputs may be any that keep to these rules, and one draw needn't show every extreme that they name: `request_adapter`: within the 64 rows of one dp index no adapter is named more than 2 times, a bound that some block reaches; every adapter is named somewhere. `adapter_storage`: A permutation of the slots.
All inputs are finite; a program needn't handle non-finite values.
Results may differ from the reference program's by a relative error of at most 0.025.
Values may be sent and summed in bfloat16 or wider, within the bound.
A program may use at most 64 MiB of HBM per device.

```python
import math
import jax
import jax.numpy as jnp
import numpy as np
from jax import lax

MODEL_WIDTH = 14848
HIDDEN_HALF = 29696
ADAPTER_RANK = 64
TOK_GRP = 64
CAP = 2
TOKENS = 2048
ADAPTER_COUNT = 64
FWB = 928
FWS = 58
N_DP = 32
N_TENSOR = 16


def block_scale(own_key, dims, shards, low, top_value):
    gain = 1.0
    for position, parts in shards:
        heights = jax.random.uniform(jax.random.fold_in(jax.random.fold_in(own_key, 6), position), (parts,), jnp.float32, low / len(shards), top_value / len(shards))
        gain = gain * jnp.repeat(jnp.exp(heights), dims[position] // parts).reshape((-1,) + (1,) * (len(dims) - 1 - position))
    return gain


def routed_block(rng, own, number, rows, count, top, bound, lean):
    sequence = jax.random.permutation(rng, count)
    heavy_load, ordinary = portions_of(count, rows * top, bound, lean, True), portions_of(count, rows * top, bound, lean, False)
    places = jnp.arange(count)

    def named(tallies, rotation):
        used = int((tallies > 0).sum())
        fixed = max(1, used // 4)
        shifted = fixed + (places - fixed + rotation * (used - fixed)) % max(1, count - fixed)
        return jnp.zeros((count,), jnp.int32).at[sequence[jnp.where(places < fixed, places, shifted)]].set(jnp.asarray(tallies, jnp.int32))

    tallies = jnp.where(number % 4 == 0, named(heavy_load, number // 4), named(ordinary, number - number // 4 - 1))
    mixed = jax.random.permutation(jax.random.fold_in(own, 3), count)
    giver, taker = mixed[0:count // 2 * 2:2], mixed[1:count // 2 * 2:2]
    margin = jnp.minimum(tallies[giver] - 1, bound - tallies[taker]) // 2
    margin = jnp.where((giver == sequence[0]) | (taker == sequence[0]) | (tallies[taker] == 0), 0, jnp.maximum(margin, 0))
    shifted = jax.random.randint(jax.random.fold_in(own, 4), (count // 2,), 0, 1 << 20) % (margin + 1)
    tallies = tallies.at[giver].add(-shifted).at[taker].add(shifted)
    labels = jnp.searchsorted(jnp.cumsum(tallies), jnp.arange(rows * top), side="right").astype(jnp.int32)
    listing = labels.reshape(top, rows).T
    listing = listing[jax.random.permutation(jax.random.fold_in(own, 1), rows)]
    rotation = jax.random.randint(jax.random.fold_in(own, 2), (rows, 1), 0, top)
    return jnp.take_along_axis(listing, (jnp.arange(top)[None, :] + rotation) % top, axis=1)


def portions_of(count, total, most, slope, full):
    loads = [(1 << 20) // math.isqrt(grade ** slope) + 1 for grade in range(1, count + 1)]
    largest = most if full else min(most, max(-(-total // count), total * loads[0] // sum(loads)))
    least = 1 if total - largest >= count - 1 else 0
    given, spare = [largest] + [least] * (count - 1), total - largest - least * (count - 1)
    while spare > 0:
        free = [i for i in range(1, count) if given[i] < largest] or [i for i in range(1, count) if given[i] < most]
        whole, remaining = sum([loads[i] for i in free]), spare
        for i in free:
            addition = min(most - given[i], max(1, remaining * loads[i] // whole), spare)
            given[i] = given[i] + addition
            spare = spare - addition
    return np.array(given)


def gaussian(stream_key, dims, width, reach, cuts=(), kind=jnp.bfloat16):
    drawn = jax.random.normal(stream_key, dims, jnp.float32) * width
    if len(cuts) > 0:
        drawn = block_scale(stream_key, dims, cuts, -0.22, 0.18) * drawn
    return jnp.clip(drawn, min=-reach, max=reach).astype(kind)


def setup_inputs(seed: int = 0) -> dict:
    arg_keys = jax.random.split(jax.random.key(seed), 7)
    tokens = gaussian(arg_keys[0], (TOKENS, MODEL_WIDTH), 1.0, 6.0, ((0, 32), (1, 16)))
    base_up_matrix = gaussian(arg_keys[1], (MODEL_WIDTH, N_DP, FWB), MODEL_WIDTH ** -0.5, 0.046875, ((0, 16), (1, 32)))
    adapter_down_maps = gaussian(arg_keys[2], (ADAPTER_COUNT, ADAPTER_RANK, MODEL_WIDTH), MODEL_WIDTH ** -0.5, 0.046875, ((0, 32), (2, 16)))
    adapter_up_maps = gaussian(arg_keys[3], (ADAPTER_COUNT, ADAPTER_RANK, HIDDEN_HALF), ADAPTER_RANK ** -0.5, 0.75, ((0, 32), (2, 16)))
    request_adapter_keys = jax.random.split(jax.random.fold_in(arg_keys[4], 1), TOKENS // TOK_GRP)
    request_adapter_turns = jax.random.permutation(jax.random.fold_in(arg_keys[4], 3), TOKENS // TOK_GRP)
    request_adapter = jax.vmap(lambda own, number: routed_block(jax.random.fold_in(arg_keys[4], 2), own, number, TOK_GRP, ADAPTER_COUNT, 1, CAP, 2))(request_adapter_keys, request_adapter_turns).reshape((TOKENS, 1))
    adapter_storage = jax.random.permutation(arg_keys[5], ADAPTER_COUNT).astype(jnp.int32)
    return {"tokens": tokens, "base_up_matrix": base_up_matrix, "adapter_down_maps": adapter_down_maps, "adapter_up_maps": adapter_up_maps, "request_adapter": request_adapter, "adapter_storage": adapter_storage}


def reference(tokens, base_up_matrix, adapter_down_maps, adapter_up_maps, request_adapter, adapter_storage):
    width_part = MODEL_WIDTH // N_TENSOR
    weight_flat = base_up_matrix.reshape(MODEL_WIDTH, HIDDEN_HALF)

    def add_part(total, index):
        start = (index * width_part).astype(jnp.int32)
        cols = lax.dynamic_slice_in_dim(tokens, start, width_part, 1)
        rows = lax.dynamic_slice_in_dim(weight_flat, start, width_part, 0)
        part = jnp.dot(cols, rows, preferred_element_type=jnp.float32).astype(jnp.bfloat16)
        part = lax.optimization_barrier(part)
        return total + part.astype(jnp.float32), None

    base, _ = lax.scan(add_part, jnp.zeros((TOKENS, HIDDEN_HALF), jnp.float32), jnp.arange(N_TENSOR, dtype=jnp.int32))
    base = base.reshape(TOKENS, N_DP, N_TENSOR, FWS).transpose(0, 2, 1, 3).reshape(TOKENS, HIDDEN_HALF)
    slot_index = adapter_storage[request_adapter[:, 0]]
    block_rows = 16
    token_blocks = tokens.reshape(TOKENS // block_rows, block_rows, MODEL_WIDTH)
    slot_blocks = slot_index.reshape(TOKENS // block_rows, block_rows)

    def adapter_block(inputs):
        token_rows, storage_rows = inputs
        down_matrix_rows = adapter_down_maps[storage_rows].astype(jnp.float32)
        reduced_state = jnp.einsum('td,trd->tr', token_rows.astype(jnp.float32), down_matrix_rows).astype(jnp.bfloat16)
        up_matrix_rows = adapter_up_maps[storage_rows].astype(jnp.float32)
        return jnp.einsum('lq,lqh->lh', reduced_state.astype(jnp.float32), up_matrix_rows).astype(jnp.bfloat16)

    delta = lax.map(adapter_block, (token_blocks, slot_blocks)).reshape(TOKENS, HIDDEN_HALF)
    return jax.nn.gelu(base + delta.astype(jnp.float32), approximate=False).astype(jnp.bfloat16)
```

```python
import jax
import jax.numpy as jnp
from jax import lax
from jax.experimental import pallas as pl
from jax.experimental.pallas import tpu as pltpu
from jax.sharding import PartitionSpec as P

MESH = pl.DeviceIdType.MESH
F32 = jnp.float32
BF16 = jnp.bfloat16

NZ = 16
NDP = 32
ROWS = 64
WIDTH = 928
WPAD = 1024
SHARE = 58
SPAD = 64
CHUNKS = 4
CTOK = 512
LAG = 2
COLS = 1856
CPAD = 1920

OFFSETS = (
    ((0, 0), (1, 0), (3, 0), (0, 1)),
    ((0, 3), (1, 1), (3, 3), (2, 0)),
    ((0, 2), (1, 3), (3, 1), (2, 1)),
    ((1, 2), (3, 2), (2, 3), (2, 2)),
)


def digits(values):
    return sum(v << (2 * i) for i, v in enumerate(values))


def pick(values, n):
    if isinstance(n, int):
        return values[n]
    return lax.rem(lax.shift_right_logical(jnp.int32(digits(values)), 2 * n), 4)


def offset(n, q):
    return pick([OFFSETS[m][q][0] for m in range(CHUNKS)], n), pick([OFFSETS[m][q][1] for m in range(CHUNKS)], n)


def dot_nt(a, b):
    return lax.dot_general(a, b, (((1,), (1,)), ((), ())), preferred_element_type=F32)


def dot_nn(a, b):
    return lax.dot_general(a, b, (((1,), (0,)), ((), ())), preferred_element_type=F32)


def iota(shape, dim):
    return lax.broadcasted_iota(jnp.int32, shape, dim)


def erf(x):
    x = jnp.clip(x, -4.0, 4.0)
    s = x * x
    p = -2.72614225801306e-10
    for c in (
        2.77068142495902e-08,
        -2.10102402082508e-06,
        -5.69250639462346e-05,
        -7.34990630326855e-04,
        -2.95459980854025e-03,
        -1.60960333262415e-02,
    ):
        p = p * s + c
    q = -1.45660718464996e-05
    for c in (-2.13374055278905e-04, -1.68282697438203e-03, -7.37332916720468e-03, -1.42647390514189e-02):
        q = q * s + c
    return x * p / q


def kernel(
    tok_ref, w_ref, down_ref, up_ref, req_ref, sto_ref, out_ref,
    xbuf, wt, y, h, lbuf, sbuf, total, rbuf, stack, sel,
    zsend, zrecv, zred, zgather, shr, shrx, dbuf, ebuf, fbuf, gbuf,
    ag_s, ag_r, fw_s, fw_r, l_s, l_r, s_s, s_r, r_s, r_r,
    z1_s, z1_r, z2_s, z2_r, e_s, e_r, g_s, g_r,
):
    dp = lax.axis_index("dp")
    z = lax.axis_index("tensor")
    core = lax.rem(dp, 2)
    cy = lax.rem(dp // 2, 4)
    cx = dp // 8
    yc = cy * 2 + core

    def dev(x, yy, c):
        return (lax.rem(x, 4) * 4 + lax.rem(yy, 4)) * 2 + c

    partner = dev(cx, cy, 1 - core)

    def remote(src, dst, ssem, rsem, target):
        return pltpu.make_async_remote_copy(
            src_ref=src, dst_ref=dst, send_sem=ssem, recv_sem=rsem, device_id=target, device_id_type=MESH
        )

    barrier = pltpu.get_barrier_semaphore()

    @pl.loop(1, NDP)
    def _(i):
        pl.semaphore_signal(barrier, inc=1, device_id=(lax.rem(dp + i, NDP), z), device_id_type=MESH)

    @pl.loop(1, NZ)
    def _(i):
        pl.semaphore_signal(barrier, inc=1, device_id=(dp, lax.rem(z + i, NZ)), device_id_type=MESH)

    onehot = req_ref[...] == iota((ROWS, 64), 1)
    slot = jnp.sum(jnp.where(onehot, sto_ref[...], 0), axis=1, keepdims=True)
    lower = (iota((ROWS, ROWS), 1) < iota((ROWS, ROWS), 0)).astype(F32).astype(BF16)
    before = dot_nn(lower, onehot.astype(F32).astype(BF16))
    rank = jnp.sum(jnp.where(onehot, before, 0.0), axis=1, keepdims=True)
    place = slot.astype(F32) * 2.0 + rank
    xbuf[0, core] = jnp.broadcast_to(place, (ROWS, WPAD)).astype(BF16)
    xbuf[0, core, :, 0:WIDTH] = tok_ref[...]

    pl.semaphore_wait(barrier, NDP - 1 + NZ - 1)

    def forward(n, q):
        p = 4 * n + q
        return remote(xbuf.at[p, core], xbuf.at[p, core], fw_s.at[p], fw_r.at[p], (partner, z))

    def gather(n, q):
        p = 4 * n + q
        dx, dy = offset(n, q)
        return remote(
            xbuf.at[0, core], xbuf.at[p, core], ag_s.at[p], ag_r.at[p], (dev(cx + dx, cy + dy, core), z)
        )

    forward(0, 0).start()
    for n in range(CHUNKS):
        for q in range(4):
            if (n, q) != (0, 0):
                gather(n, q).start()

    wt[...] = jnp.zeros_like(wt)

    @pl.loop(0, 4)
    def _(b):
        row = iota((256, WIDTH), 0)
        unit = (b * 4 + row // SPAD) * SHARE + row % SPAD
        pickrow = jnp.where((row % SPAD < SHARE) & (unit == iota((256, WIDTH), 1)), 1.0, 0.0).astype(BF16)
        wt[b, :, 0:WIDTH] = dot_nt(pickrow, w_ref[...]).astype(BF16)

    wt[4, 0:128, 0:WIDTH] = down_ref[...]
    dbuf[...] = jnp.zeros_like(dbuf)

    def relay(n):
        for q in range(4):

            @pl.when(n * 4 + q > 0)
            def _():
                gather(n, q).wait_recv()
                forward(n, q).start()

    def multiply(n):
        for q in range(4):
            p = 4 * n + q
            remote(xbuf.at[p, 1 - core], xbuf.at[p, 1 - core], fw_s.at[p], fw_r.at[p], (partner, z)).wait_recv()

        @pl.loop(0, 4)
        def _(b):
            x = xbuf[pl.ds(4 * n, 4)].reshape(CTOK, WPAD)
            y[n, pl.ds(4 * b, 4)] = dot_nt(wt[b], x).reshape(4, SPAD, CTOK).astype(BF16)

        x = xbuf[pl.ds(4 * n, 4)].reshape(CTOK, WPAD)
        low = dot_nt(wt[4, 0:128], x).astype(BF16)
        for q in range(4):
            h[4 * n + q] = low[:, q * 128 : (q + 1) * 128]

    def long_hop(n, s, src):
        way = 1 - 2 * lax.rem(n, 2)
        return remote(src, lbuf.at[n, s], l_s.at[n, s], l_r.at[n, s], (dp, lax.rem(z + way + NZ, NZ)))

    def short_hop(n, s, src):
        way = 1 - 2 * lax.rem(n, 2)
        return remote(src, sbuf.at[n, s], s_s.at[n, s], s_r.at[n, s], (dp, lax.rem(z - way + NZ, NZ)))

    def long_target(n, s):
        return lax.rem(z + (1 - 2 * lax.rem(n, 2)) * (8 - s) + NZ, NZ)

    def short_target(n, s):
        return lax.rem(z - (1 - 2 * lax.rem(n, 2)) * (7 - s) + NZ, NZ)

    def result(n, q, c):
        dx, dy = offset(n, q)
        target = dev(cx + 4 - dx, cy + 4 - dy, c)
        return remote(total.at[n, q], rbuf.at[dp], r_s.at[n, q, c], r_r.at[n, q, core], (target, z))

    def result_arrives(n, q, c):
        dx, dy = offset(n, q)
        source = dev(cx + dx, cy + dy, c)
        return remote(total.at[n, q], rbuf.at[source], r_s.at[n, q, c], r_r.at[n, q, c], (partner, z))

    def stage(n, s):
        @pl.when(s == 0)
        def _():
            multiply(n)
            long_hop(n, 0, y.at[n, long_target(n, 0)]).start()
            short_hop(n, 0, y.at[n, short_target(n, 0)]).start()

        @pl.when((s >= 1) & (s <= 7))
        def _():
            here = lbuf.at[n, s - 1]
            long_hop(n, s - 1, here).wait_recv()
            lbuf[n, s - 1] = (lbuf[n, s - 1].astype(F32) + y[n, long_target(n, s)].astype(F32)).astype(BF16)
            long_hop(n, s, here).start()

        @pl.when((s >= 1) & (s <= 6))
        def _():
            here = sbuf.at[n, s - 1]
            short_hop(n, s - 1, here).wait_recv()
            sbuf[n, s - 1] = (sbuf[n, s - 1].astype(F32) + y[n, short_target(n, s)].astype(F32)).astype(BF16)
            short_hop(n, s, here).start()

        @pl.when(s == 8)
        def _():
            short_hop(n, 6, sbuf.at[n, 6]).wait_recv()
            long_hop(n, 7, lbuf.at[n, 7]).wait_recv()
            both = lbuf[n, 7].astype(F32) + sbuf[n, 6].astype(F32) + y[n, z].astype(F32)
            both = both.astype(BF16)
            for q in range(4):
                total[n, q] = both[:, q * 128 : (q + 1) * 128]
            for q in range(4):
                for c in range(2):

                    @pl.when((n > 0) | (q > 0) | (core != c))
                    def _():
                        result(n, q, c).start()

            @pl.when(n == 0)
            def _():
                rbuf[dp] = total[0, 0]

    def tick(t):
        for n in range(CHUNKS):

            @pl.when(t == max(0, LAG * n - 1))
            def _():
                relay(n)

        @pl.loop(0, CHUNKS)
        def _(n):
            s = t - LAG * n

            @pl.when((s >= 0) & (s <= 8))
            def _():
                stage(n, s)

    lane64 = iota((64, 128), 1)

    def shrink():
        key = dp * 4

        @pl.loop(0, 16)
        def _(p):
            n, q = p // 4, p % 4
            dx = pick([OFFSETS[m][0][0] for m in range(4)], n)
            dy = pick([OFFSETS[m][0][1] for m in range(4)], n)
            for j in range(1, 4):
                ox, oy = offset(n, j)
                dx = jnp.where(q == j, ox, dx)
                dy = jnp.where(q == j, oy, dy)
            x = lax.rem(cx + 4 - dx, 4)
            yy = lax.rem(cy + 4 - dy, 4)
            meta = dot_nt(
                jnp.where(iota((16, 128), 1) == 127, 1.0, 0.0).astype(BF16),
                xbuf[p, :, :, WPAD - 128 : WPAD].reshape(128, 128),
            )[0:1]
            row = iota((128, 128), 0)
            home = (yy * 2 + iota((128, 128), 1) // 64) * 4 + x
            wanted = key + 2 * (row // 64) + row % 2
            hit = ((row % 64) // 2 == home) & (meta.astype(jnp.int32) == wanted)
            sel[p] = jnp.where(hit, 1.0, 0.0).astype(BF16)

        acc = jnp.zeros((128, 128), F32)
        for p in range(16):
            acc = acc + dot_nt(sel[p], h[p])
        part = jnp.where(lane64 < 64, acc[0:64], acc[64:128])
        for i in range(NZ):
            zsend[i] = part[4 * i : 4 * i + 4]

        @pl.loop(1, NZ)
        def _(i):
            other = lax.rem(z + i, NZ)
            remote(zsend.at[other], zrecv.at[z], z1_s.at[i], z1_r.at[i], (dp, other)).start()

        zrecv[z] = zsend[z]

    def reduce():
        @pl.loop(1, NZ)
        def _(i):
            other = lax.rem(z + NZ - i, NZ)
            remote(zsend.at[other], zrecv.at[other], z1_s.at[i], z1_r.at[i], (dp, other)).wait_recv()

        whole = zrecv[0]
        for i in range(1, NZ):
            whole = whole + zrecv[i]
        zred[...] = whole

        @pl.loop(1, NZ)
        def _(i):
            other = lax.rem(z + i, NZ)
            remote(zred, zgather.at[z], z2_s.at[i], z2_r.at[i], (dp, other)).start()

        zgather[z] = zred[...]

    def grow():
        @pl.loop(1, NZ)
        def _(i):
            other = lax.rem(z + NZ - i, NZ)
            remote(zred, zgather.at[other], z2_s.at[i], z2_r.at[i], (dp, other)).wait_recv()

        for i in range(NZ):
            shr[4 * i : 4 * i + 4] = zgather[i]
        rows = shr[...]
        for g in range(8):
            eight = rows[8 * g : 8 * g + 8]
            lane = lane64[0:8]
            shrx[16 * g : 16 * g + 8] = jnp.where(lane < 64, eight, 0.0)
            shrx[16 * g + 8 : 16 * g + 16] = jnp.where(lane < 64, 0.0, eight)
        grown = dot_nn(shrx[...].astype(BF16), up_ref[...])
        dbuf[:, :, 0:COLS] = grown.reshape(8, 16, COLS).astype(BF16)

        @pl.loop(1, 8)
        def _(i):
            other = lax.rem(yc + i, 8)
            target = dev(cx, other // 2, lax.rem(other, 2))
            remote(dbuf.at[other], ebuf.at[yc], e_s.at[i], e_r.at[i], (target, z)).start()

        ebuf[yc] = dbuf[yc]

    def sort():
        @pl.loop(1, 8)
        def _(i):
            other = lax.rem(yc + 8 - i, 8)
            target = dev(cx, other // 2, lax.rem(other, 2))
            remote(dbuf.at[other], ebuf.at[other], e_s.at[i], e_r.at[i], (target, z)).wait_recv()

        to = iota((128, 128), 0)
        source = ((to // 4) % 8) * 16 + ((to // 2) % 2) * 8 + (to // 32) * 2 + to % 2
        perm = jnp.where(iota((128, 128), 1) == source, 1.0, 0.0).astype(BF16)
        fbuf[...] = dot_nn(perm, ebuf[...].reshape(128, CPAD)).reshape(4, 32, CPAD).astype(BF16)

        @pl.loop(1, 4)
        def _(i):
            other = lax.rem(cx + i, 4)
            remote(fbuf.at[other], gbuf.at[cx], g_s.at[i], g_r.at[i], (dev(other, cy, core), z)).start()

        gbuf[cx] = fbuf[cx]

    def deltas():
        @pl.loop(1, 4)
        def _(i):
            other = lax.rem(cx + 4 - i, 4)
            remote(fbuf.at[other], gbuf.at[other], g_s.at[i], g_r.at[i], (dev(other, cy, core), z)).wait_recv()

        mine = (place.astype(jnp.int32) == iota((ROWS, 128), 1)).astype(F32).astype(BF16)
        return dot_nn(mine, gbuf[...].reshape(128, CPAD))[:, 0:COLS]

    last = LAG * (CHUNKS - 1) + 8
    full = LAG * (CHUNKS - 1)

    steps = ((full + 1, shrink), (full + 3, reduce), (full + 5, grow), (full + 7, sort))
    done = 0
    for until, what in steps:

        @pl.loop(done, until)
        def _(t):
            tick(t)

        what()
        done = until

    @pl.loop(done, last + 1)
    def _(t):
        tick(t)

    delta = deltas()

    @pl.loop(0, CHUNKS)
    def _(n):
        for q in range(4):
            for c in range(2):

                @pl.when((n > 0) | (q > 0) | (core != c))
                def _():
                    result_arrives(n, q, c).wait_recv()

    for k in range(NDP):
        stack[k * SHARE : (k + 1) * SHARE] = rbuf[k].astype(F32)[0:SHARE]
    turn = jnp.where(iota((ROWS, 128), 1) == core * 64 + iota((ROWS, 128), 0), 1.0, 0.0).astype(BF16)
    base = dot_nt(turn, stack[...].astype(BF16))
    v = base + delta
    out_ref[...] = (0.5 * v * (1.0 + erf(v * 0.7071067811865476))).astype(BF16)

    @pl.loop(0, CHUNKS)
    def _(n):
        for q in range(4):
            forward(n, q).wait_send()

            @pl.when(n * 4 + q > 0)
            def _():
                gather(n, q).wait_send()

            for c in range(2):

                @pl.when((n > 0) | (q > 0) | (core != c))
                def _():
                    result(n, q, c).wait_send()

        @pl.loop(0, 8)
        def _(s):
            long_hop(n, s, lbuf.at[n, s]).wait_send()

        @pl.loop(0, 7)
        def _(s):
            short_hop(n, s, sbuf.at[n, s]).wait_send()

    @pl.loop(1, NZ)
    def _(i):
        other = lax.rem(z + i, NZ)
        remote(zsend.at[other], zrecv.at[z], z1_s.at[i], z1_r.at[i], (dp, other)).wait_send()
        remote(zred, zgather.at[z], z2_s.at[i], z2_r.at[i], (dp, other)).wait_send()

    @pl.loop(1, 8)
    def _(i):
        remote(dbuf.at[yc], ebuf.at[yc], e_s.at[i], e_r.at[i], (partner, z)).wait_send()

    @pl.loop(1, 4)
    def _(i):
        remote(fbuf.at[cx], gbuf.at[cx], g_s.at[i], g_r.at[i], (partner, z)).wait_send()


def local(tokens, base_up_matrix, adapter_down_maps, adapter_up_maps, request_adapter, adapter_storage):
    dma = pltpu.SemaphoreType.DMA
    vmem = pl.BlockSpec(memory_space=pltpu.VMEM)
    return pl.pallas_call(
        kernel,
        out_shape=jax.ShapeDtypeStruct((ROWS, COLS), BF16),
        in_specs=[vmem] * 6,
        out_specs=vmem,
        scratch_shapes=[
            pltpu.VMEM((16, 2, ROWS, WPAD), BF16),
            pltpu.VMEM((5, 256, WPAD), BF16),
            pltpu.VMEM((CHUNKS, NZ, SPAD, CTOK), BF16),
            pltpu.VMEM((16, 128, 128), BF16),
            pltpu.VMEM((CHUNKS, 8, SPAD, CTOK), BF16),
            pltpu.VMEM((CHUNKS, 7, SPAD, CTOK), BF16),
            pltpu.VMEM((CHUNKS, 4, SPAD, 128), BF16),
            pltpu.VMEM((NDP, SPAD, 128), BF16),
            pltpu.VMEM((COLS, 128), F32),
            pltpu.VMEM((16, 128, 128), BF16),
            pltpu.VMEM((NZ, 4, 128), F32),
            pltpu.VMEM((NZ, 4, 128), F32),
            pltpu.VMEM((4, 128), F32),
            pltpu.VMEM((NZ, 4, 128), F32),
            pltpu.VMEM((64, 128), F32),
            pltpu.VMEM((128, 128), F32),
            pltpu.VMEM((8, 16, CPAD), BF16),
            pltpu.VMEM((8, 16, CPAD), BF16),
            pltpu.VMEM((4, 32, CPAD), BF16),
            pltpu.VMEM((4, 32, CPAD), BF16),
            dma((16,)), dma((16,)), dma((16,)), dma((16,)),
            dma((CHUNKS, 8)), dma((CHUNKS, 8)), dma((CHUNKS, 7)), dma((CHUNKS, 7)),
            dma((CHUNKS, 4, 2)), dma((CHUNKS, 4, 2)),
            dma((NZ,)), dma((NZ,)), dma((NZ,)), dma((NZ,)),
            dma((8,)), dma((8,)), dma((4,)), dma((4,)),
        ],
        compiler_params=pltpu.CompilerParams(
            collective_id=0, has_side_effects=True, vmem_limit_bytes=56 * 1024 * 1024
        ),
        name="gather_sum_exchange",
    )(
        tokens,
        base_up_matrix.reshape(WIDTH, WIDTH),
        adapter_down_maps.reshape(128, WIDTH),
        adapter_up_maps.reshape(128, COLS),
        request_adapter,
        adapter_storage.reshape(1, 64),
    )


def solution(mesh):
    return jax.shard_map(
        local,
        mesh=mesh,
        in_specs=(
            P("dp", "tensor"),
            P("tensor", "dp", None),
            P("dp", None, "tensor"),
            P("dp", None, "tensor"),
            P("dp", None),
            P(),
        ),
        out_specs=P("dp", "tensor"),
        check_vma=False,
    )
```

```python
import jax
import jax.numpy as jnp
from jax import lax
from jax.experimental import pallas as pl
from jax.experimental.pallas import tpu as pltpu
from jax.sharding import PartitionSpec as P

MESH = pl.DeviceIdType.MESH
F32 = jnp.float32
BF16 = jnp.bfloat16

NZ = 16
NDP = 32
ROWS = 64
WIDTH = 928
WPAD = 1024
SHARE = 58
SPAD = 64
CHUNKS = 4
CTOK = 512
CROWS = 240
COLS = 1856
CPAD = 1920

OFFSETS = (
    ((0, 0), (1, 0), (3, 0), (0, 1)),
    ((0, 3), (1, 1), (1, 3), (3, 1)),
    ((3, 3), (2, 0), (0, 2), (2, 1)),
    ((2, 3), (1, 2), (3, 2), (2, 2)),
)
POS = {offset: 4 * n + q for n, chunk in enumerate(OFFSETS) for q, offset in enumerate(chunk)}

PARTS = tuple(
    [(1, 0, "F"), (3, 0, "F"), (2, 0, "a"), (2, 0, "b")]
    + [(f, g, part) for f in range(4) for g, part in ((1, "F"), (3, "F"), (2, "a"), (2, "b"))]
)

ORDER = (
    "w0", "w1", "w2", "w3", "10F", "30F", "01F", "03F", "20a", "m00",
    "13F", "s00", "11F", "20b", "m01", "m02", "m03", "31F", "33F", "02a",
    "02b", "l0", "s01", "12b", "12a", "m10", "s10", "m11", "21F", "23F",
    "m12", "32a", "32b", "m13", "s02", "m20", "s20", "22a", "22b", "s11",
    "m21", "m22", "m23", "m30", "s30", "s03", "m31", "m32", "s21", "m33",
    "l1", "s12", "l2", "l3", "shrink", "s31", "s22", "s13", "s32", "s23",
    "s14", "reduce", "s33", "s24", "s04", "s34", "s25", "s15", "grow", "s35",
    "s05", "s26", "s36", "s16", "s06", "sort", "s37", "s27", "s17", "s07",
    "s38", "s28", "delta", "s18", "s08",
)


def dot_nt(a, b):
    return lax.dot_general(a, b, (((1,), (1,)), ((), ())), preferred_element_type=F32)


def dot_nn(a, b):
    return lax.dot_general(a, b, (((1,), (0,)), ((), ())), preferred_element_type=F32)


def iota(shape, dim):
    return lax.broadcasted_iota(jnp.int32, shape, dim)


def erf(x):
    x = jnp.clip(x, -4.0, 4.0)
    s = x * x
    p = -2.72614225801306e-10
    for c in (
        2.77068142495902e-08,
        -2.10102402082508e-06,
        -5.69250639462346e-05,
        -7.34990630326855e-04,
        -2.95459980854025e-03,
        -1.60960333262415e-02,
    ):
        p = p * s + c
    q = -1.45660718464996e-05
    for c in (-2.13374055278905e-04, -1.68282697438203e-03, -7.37332916720468e-03, -1.42647390514189e-02):
        q = q * s + c
    return x * p / q


def kernel(
    tok_ref, w_any, down_any, up_any, req_ref, sto_ref, out_ref,
    w_ref, down_ref, up_ref, xbuf, wt, low, ylong, yshort, first, h, lbuf, sbuf, both, total, rbuf, stack, sel,
    zsend, zrecv, zred, zgather, shr, shrx, dbuf, ebuf, fbuf, gbuf, dterm,
    in_s, ag_s, ag_r, fw_s, fw_r, l_s, l_r, s_s, s_r, r_s, r_r,
    z1_s, z1_r, z2_s, z2_r, e_s, e_r, g_s, g_r,
):
    dp = lax.axis_index("dp")
    z = lax.axis_index("tensor")
    core = lax.rem(dp, 2)
    cy = lax.rem(dp // 2, 4)
    cx = dp // 8
    yc = cy * 2 + core
    way = 1 - 2 * core

    def dev(x, yy, c):
        return (lax.rem(x, 4) * 4 + lax.rem(yy, 4)) * 2 + c

    partner = dev(cx, cy, 1 - core)
    steps = {
        ("f", 1): dev(cx + core, cy + 1 - core, core),
        ("f", 3): dev(cx + 3 * core, cy + 3 * (1 - core), core),
        ("g", 1): dev(cx + 1 - core, cy + core, core),
        ("g", 3): dev(cx + 3 * (1 - core), cy + 3 * core, core),
    }

    def remote(src, dst, ssem, rsem, target):
        return pltpu.make_async_remote_copy(
            src_ref=src, dst_ref=dst, send_sem=ssem, recv_sem=rsem, device_id=target, device_id_type=MESH
        )

    barrier = pltpu.get_barrier_semaphore()

    @pl.loop(1, NZ)
    def _(i):
        pl.semaphore_signal(barrier, inc=1, device_id=(dp, lax.rem(z + i, NZ)), device_id_type=MESH)

    @pl.loop(1, NDP)
    def _(i):
        pl.semaphore_signal(barrier, inc=1, device_id=(lax.rem(dp + i, NDP), z), device_id_type=MESH)

    loads = {
        "w": pltpu.make_async_copy(w_any, w_ref, in_s.at[0]),
        "down": pltpu.make_async_copy(down_any, down_ref, in_s.at[1]),
        "up": pltpu.make_async_copy(up_any, up_ref, in_s.at[2]),
    }
    for load in loads.values():
        load.start()

    diagonal = iota((ROWS, ROWS), 0) == iota((ROWS, ROWS), 1)
    adapter = jnp.sum(jnp.where(diagonal, req_ref[...], 0), axis=1, keepdims=True)
    onehot = adapter == iota((ROWS, 64), 1)
    slot = jnp.sum(jnp.where(onehot, sto_ref[...], 0), axis=1, keepdims=True)
    lower = (iota((ROWS, ROWS), 1) < iota((ROWS, ROWS), 0)).astype(F32).astype(BF16)
    before = dot_nn(lower, onehot.astype(F32).astype(BF16))
    rank = jnp.sum(jnp.where(onehot, before, 0.0), axis=1, keepdims=True)
    place = slot.astype(F32) * 2.0 + rank
    xbuf[0, core, :, WPAD - 128 : WPAD] = jnp.broadcast_to(place, (ROWS, 128)).astype(BF16)
    xbuf[0, core, :, 0:WIDTH] = tok_ref[...]

    pl.semaphore_wait(barrier, NDP - 1 + NZ - 1)

    def where_at(f, g):
        return POS[g, f] + core * (POS[f, g] - POS[g, f])

    def part_copy(f, g, part):
        axis, d = ("f", f) if g == 0 else ("g", g)
        if part == "F":
            start, size, back, way_on = 0, ROWS, d, d
        else:
            start, size = (0, ROWS // 2) if part == "a" else (ROWS // 2, ROWS // 2)
            back = way_on = 1 if part == "a" else 3
        if part == "F":
            source = (0, 0) if g == 0 else (f, 0)
        else:
            source = (back, 0) if g == 0 else (f, back)
        i = PARTS.index((f, g, part))
        rows = pl.ds(start, size)
        return remote(
            xbuf.at[where_at(*source), core, rows], xbuf.at[where_at(f, g), core, rows],
            ag_s.at[i], ag_r.at[i], (steps[axis, way_on], z),
        )

    def forward(p):
        return remote(xbuf.at[p, core], xbuf.at[p, core], fw_s.at[p], fw_r.at[p], (partner, z))

    for part in ((1, 0, "F"), (3, 0, "F"), (0, 1, "F"), (0, 3, "F")):
        part_copy(*part).start()
    forward(0).start()

    low[...] = jnp.zeros_like(low)
    dbuf[...] = jnp.zeros_like(dbuf)
    ylong[:, :, CROWS - 8 : CROWS] = jnp.zeros((CHUNKS, 8, 8, 128), F32)
    yshort[:, :, CROWS - 8 : CROWS] = jnp.zeros((CHUNKS, 8, 8, 128), F32)

    arrived = {}

    def gathered(f, g, part):
        part_copy(f, g, part).wait_recv()
        if part == "F":
            half = "a" if (f if g == 0 else g) == 1 else "b"
            part_copy(2, 0, half).start() if g == 0 else part_copy(f, 2, half).start()
        else:
            arrived[f, g] = arrived.get((f, g), 0) + 1
            if arrived[f, g] < 2:
                return
        forward(where_at(f, g)).start()
        if g == 0:
            part_copy(f, 1, "F").start()
            part_copy(f, 3, "F").start()

    def offsets(b):
        return (8 - 2 * b, 9 + 2 * b, 7 - 2 * b, 10 + 2 * b)

    def weights(b):
        if b == 0:
            loads["w"].wait()
        row = iota((256, WIDTH), 0)
        plane = jnp.zeros((256, WIDTH), jnp.int32)
        for j, o in enumerate(offsets(b)):
            plane = jnp.where(row // SPAD == j, lax.rem(z + way * o + NZ, NZ), plane)
        unit = plane * SHARE + row % SPAD
        pickrow = jnp.where((row % SPAD < SHARE) & (unit == iota((256, WIDTH), 1)), 1.0, 0.0).astype(BF16)
        wt[b, :, WPAD - 128 : WPAD] = jnp.zeros((256, 128), BF16)
        wt[b, :, 0:WIDTH] = dot_nt(pickrow, w_ref[...]).astype(BF16)
        if b == 3:
            loads["down"].wait()
            low[:, 0:WIDTH] = down_ref[...]

    def multiply(n, b):
        if b == 0:
            for q in range(4):
                p = 4 * n + q
                remote(xbuf.at[p, 1 - core], xbuf.at[p, 1 - core], fw_s.at[p], fw_r.at[p], (partner, z)).wait_recv()
        x = xbuf[4 * n : 4 * n + 4].reshape(CTOK, WPAD)
        part = dot_nt(wt[b], x)
        for j in range(4):
            dest, s = (ylong, yshort)[j % 2], 2 * b + j // 2
            for q in range(4):
                dest[n, s, q * SHARE : (q + 1) * SHARE] = part[j * SPAD : j * SPAD + SHARE, q * 128 : (q + 1) * 128]

    def down(n):
        x = xbuf[4 * n : 4 * n + 4].reshape(CTOK, WPAD)
        part = dot_nt(low[...], x).astype(BF16)
        for q in range(4):
            h[4 * n + q] = part[:, q * 128 : (q + 1) * 128]

    def long_hop(n, s, src):
        return remote(src, lbuf.at[n, s], l_s.at[n, s], l_r.at[n, s], (dp, lax.rem(z + way + NZ, NZ)))

    def short_hop(n, s, src):
        return remote(src, sbuf.at[n, s], s_s.at[n, s], s_r.at[n, s], (dp, lax.rem(z - way + NZ, NZ)))

    def result(n, q, c):
        dx, dy = OFFSETS[n][q]
        target = dev(cx + 4 - dx, cy + 4 - dy, c)
        return remote(total.at[n, q], rbuf.at[dp], r_s.at[n, q, c], r_r.at[n, q, core], (target, z))

    def result_arrives(n, q, c):
        dx, dy = OFFSETS[n][q]
        source = dev(cx + dx, cy + dy, c)
        return remote(total.at[n, q], rbuf.at[source], r_s.at[n, q, c], r_r.at[n, q, c], (partner, z))

    def others(n, q, c, what):
        if n == 0 and q == 0:

            @pl.when(core != c)
            def _():
                what(n, q, c)

        else:
            what(n, q, c)

    def stage(n, s):
        if s == 0:
            first[n, 0] = ylong[n, 0].astype(BF16)
            long_hop(n, 0, first.at[n, 0]).start()
            first[n, 1] = yshort[n, 0].astype(BF16)
            short_hop(n, 0, first.at[n, 1]).start()
        if 1 <= s <= 7:
            here = lbuf.at[n, s - 1]
            long_hop(n, s - 1, here).wait_recv()
            lbuf[n, s - 1] = (lbuf[n, s - 1].astype(F32) + ylong[n, s]).astype(BF16)
            long_hop(n, s, here).start()
        if 1 <= s <= 6:
            here = sbuf.at[n, s - 1]
            short_hop(n, s - 1, here).wait_recv()
            sbuf[n, s - 1] = (sbuf[n, s - 1].astype(F32) + yshort[n, s]).astype(BF16)
            short_hop(n, s, here).start()
        if s == 8:
            short_hop(n, 6, sbuf.at[n, 6]).wait_recv()
            long_hop(n, 7, lbuf.at[n, 7]).wait_recv()
            both[...] = lbuf[n, 7].astype(F32) + sbuf[n, 6].astype(F32) + yshort[n, 7]
            for q in range(4):
                total[n, q] = both[q * SHARE : q * SHARE + SPAD].astype(BF16)
                for c in range(2):
                    others(n, q, c, lambda *a: result(*a).start())
            if n == 0:
                rbuf[dp] = total[0, 0]

    lane64 = iota((64, 128), 1)

    def shrink():
        key = dp * 4
        for n in range(CHUNKS):
            for q in range(4):
                p = 4 * n + q
                dx, dy = OFFSETS[n][q]
                x = lax.rem(cx + 4 - dx, 4)
                yy = lax.rem(cy + 4 - dy, 4)
                meta = dot_nt(
                    jnp.where(iota((16, 128), 1) == 127, 1.0, 0.0).astype(BF16),
                    xbuf[p, :, :, WPAD - 128 : WPAD].reshape(128, 128),
                )[0:1]
                row = iota((128, 128), 0)
                home = (yy * 2 + iota((128, 128), 1) // 64) * 4 + x
                wanted = key + 2 * (row // 64) + row % 2
                hit = ((row % 64) // 2 == home) & (meta.astype(jnp.int32) == wanted)
                sel[p] = jnp.where(hit, 1.0, 0.0).astype(BF16)
        acc = jnp.zeros((128, 128), F32)
        for p in range(16):
            acc = acc + dot_nt(sel[p], h[p])
        part = jnp.where(lane64 < 64, acc[0:64], acc[64:128])
        for i in range(NZ):
            zsend[i] = part[4 * i : 4 * i + 4]

        @pl.loop(1, NZ)
        def _(i):
            other = lax.rem(z + i, NZ)
            remote(zsend.at[other], zrecv.at[z], z1_s.at[i], z1_r.at[i], (dp, other)).start()

        zrecv[z] = zsend[z]

    def reduce():
        @pl.loop(1, NZ)
        def _(i):
            other = lax.rem(z + NZ - i, NZ)
            remote(zsend.at[other], zrecv.at[other], z1_s.at[i], z1_r.at[i], (dp, other)).wait_recv()

        whole = zrecv[0]
        for i in range(1, NZ):
            whole = whole + zrecv[i]
        zred[...] = whole

        @pl.loop(1, NZ)
        def _(i):
            other = lax.rem(z + i, NZ)
            remote(zred, zgather.at[z], z2_s.at[i], z2_r.at[i], (dp, other)).start()

        zgather[z] = zred[...]

    def grow():
        @pl.loop(1, NZ)
        def _(i):
            other = lax.rem(z + NZ - i, NZ)
            remote(zred, zgather.at[other], z2_s.at[i], z2_r.at[i], (dp, other)).wait_recv()

        for i in range(NZ):
            shr[4 * i : 4 * i + 4] = zgather[i]
        rows = shr[...]
        for g in range(8):
            eight = rows[8 * g : 8 * g + 8]
            lane = lane64[0:8]
            shrx[16 * g : 16 * g + 8] = jnp.where(lane < 64, eight, 0.0)
            shrx[16 * g + 8 : 16 * g + 16] = jnp.where(lane < 64, 0.0, eight)
        loads["up"].wait()
        grown = dot_nn(shrx[...].astype(BF16), up_ref[...])
        dbuf[:, :, 0:COLS] = grown.reshape(8, 16, COLS).astype(BF16)

        @pl.loop(1, 8)
        def _(i):
            other = lax.rem(yc + i, 8)
            target = dev(cx, other // 2, lax.rem(other, 2))
            remote(dbuf.at[other], ebuf.at[yc], e_s.at[i], e_r.at[i], (target, z)).start()

        ebuf[yc] = dbuf[yc]

    def sort():
        @pl.loop(1, 8)
        def _(i):
            other = lax.rem(yc + 8 - i, 8)
            target = dev(cx, other // 2, lax.rem(other, 2))
            remote(dbuf.at[other], ebuf.at[other], e_s.at[i], e_r.at[i], (target, z)).wait_recv()

        to = iota((128, 128), 0)
        source = ((to // 4) % 8) * 16 + ((to // 2) % 2) * 8 + (to // 32) * 2 + to % 2
        perm = jnp.where(iota((128, 128), 1) == source, 1.0, 0.0).astype(BF16)
        fbuf[...] = dot_nn(perm, ebuf[...].reshape(128, CPAD)).reshape(4, 32, CPAD).astype(BF16)

        @pl.loop(1, 4)
        def _(i):
            other = lax.rem(cx + i, 4)
            remote(fbuf.at[other], gbuf.at[cx], g_s.at[i], g_r.at[i], (dev(other, cy, core), z)).start()

        gbuf[cx] = fbuf[cx]

    def deltas():
        @pl.loop(1, 4)
        def _(i):
            other = lax.rem(cx + 4 - i, 4)
            remote(fbuf.at[other], gbuf.at[other], g_s.at[i], g_r.at[i], (dev(other, cy, core), z)).wait_recv()

        mine = (place.astype(jnp.int32) == iota((ROWS, 128), 1)).astype(F32).astype(BF16)
        dterm[...] = dot_nn(mine, gbuf[...].reshape(128, CPAD))[:, 0:COLS]

    adapters = {"shrink": shrink, "reduce": reduce, "grow": grow, "sort": sort, "delta": deltas}
    for word in ORDER:
        if word in adapters:
            adapters[word]()
        elif word[0] == "w":
            weights(int(word[1]))
        elif word[0] == "m":
            multiply(int(word[1]), int(word[2]))
        elif word[0] == "s":
            stage(int(word[1]), int(word[2]))
        elif word[0] == "l":
            down(int(word[1]))
        else:
            gathered(int(word[0]), int(word[1]), word[2])

    for part in PARTS:
        if part != (0, 0, "F"):
            part_copy(*part).wait_send()
    for p in range(16):
        forward(p).wait_send()
    for n in range(CHUNKS):
        for s in range(8):
            long_hop(n, s, lbuf.at[n, s]).wait_send()
        for s in range(7):
            short_hop(n, s, sbuf.at[n, s]).wait_send()

    @pl.loop(1, NZ)
    def _(i):
        other = lax.rem(z + i, NZ)
        remote(zsend.at[other], zrecv.at[z], z1_s.at[i], z1_r.at[i], (dp, other)).wait_send()
        remote(zred, zgather.at[z], z2_s.at[i], z2_r.at[i], (dp, other)).wait_send()

    @pl.loop(1, 8)
    def _(i):
        remote(dbuf.at[yc], ebuf.at[yc], e_s.at[i], e_r.at[i], (partner, z)).wait_send()

    @pl.loop(1, 4)
    def _(i):
        remote(fbuf.at[cx], gbuf.at[cx], g_s.at[i], g_r.at[i], (partner, z)).wait_send()

    for n in range(CHUNKS):
        for q in range(4):
            for c in range(2):
                others(n, q, c, lambda *a: result(*a).wait_send())
    for n in range(CHUNKS):
        for q in range(4):
            for c in range(2):
                others(n, q, c, lambda *a: result_arrives(*a).wait_recv())

    for k in range(NDP):
        stack[k * SHARE : (k + 1) * SHARE] = rbuf[k].astype(F32)[0:SHARE]
    turn = jnp.where(iota((ROWS, 128), 1) == core * 64 + iota((ROWS, 128), 0), 1.0, 0.0).astype(BF16)
    v = dot_nt(turn, stack[...].astype(BF16)) + dterm[...]
    out_ref[...] = (0.5 * v * (1.0 + erf(v * 0.7071067811865476))).astype(BF16)


def local(tokens, base_up_matrix, adapter_down_maps, adapter_up_maps, request_adapter, adapter_storage):
    dma = pltpu.SemaphoreType.DMA
    vmem = pl.BlockSpec(memory_space=pltpu.VMEM)
    hbm = pl.BlockSpec(memory_space=pl.ANY)
    return pl.pallas_call(
        kernel,
        out_shape=jax.ShapeDtypeStruct((ROWS, COLS), BF16),
        in_specs=[vmem, hbm, hbm, hbm, vmem, vmem],
        out_specs=vmem,
        scratch_shapes=[
            pltpu.VMEM((WIDTH, WIDTH), BF16),
            pltpu.VMEM((128, WIDTH), BF16),
            pltpu.VMEM((128, COLS), BF16),
            pltpu.VMEM((16, 2, ROWS, WPAD), BF16),
            pltpu.VMEM((4, 256, WPAD), BF16),
            pltpu.VMEM((128, WPAD), BF16),
            pltpu.VMEM((CHUNKS, 8, CROWS, 128), F32),
            pltpu.VMEM((CHUNKS, 8, CROWS, 128), F32),
            pltpu.VMEM((CHUNKS, 2, CROWS, 128), BF16),
            pltpu.VMEM((16, 128, 128), BF16),
            pltpu.VMEM((CHUNKS, 8, CROWS, 128), BF16),
            pltpu.VMEM((CHUNKS, 7, CROWS, 128), BF16),
            pltpu.VMEM((CROWS, 128), F32),
            pltpu.VMEM((CHUNKS, 4, SPAD, 128), BF16),
            pltpu.VMEM((NDP, SPAD, 128), BF16),
            pltpu.VMEM((COLS, 128), F32),
            pltpu.VMEM((16, 128, 128), BF16),
            pltpu.VMEM((NZ, 4, 128), F32),
            pltpu.VMEM((NZ, 4, 128), F32),
            pltpu.VMEM((4, 128), F32),
            pltpu.VMEM((NZ, 4, 128), F32),
            pltpu.VMEM((64, 128), F32),
            pltpu.VMEM((128, 128), F32),
            pltpu.VMEM((8, 16, CPAD), BF16),
            pltpu.VMEM((8, 16, CPAD), BF16),
            pltpu.VMEM((4, 32, CPAD), BF16),
            pltpu.VMEM((4, 32, CPAD), BF16),
            pltpu.VMEM((ROWS, COLS), F32),
            dma((3,)), dma((len(PARTS),)), dma((len(PARTS),)), dma((16,)), dma((16,)),
            dma((CHUNKS, 8)), dma((CHUNKS, 8)), dma((CHUNKS, 7)), dma((CHUNKS, 7)),
            dma((CHUNKS, 4, 2)), dma((CHUNKS, 4, 2)),
            dma((NZ,)), dma((NZ,)), dma((NZ,)), dma((NZ,)),
            dma((8,)), dma((8,)), dma((4,)), dma((4,)),
        ],
        compiler_params=pltpu.CompilerParams(
            collective_id=0, has_side_effects=True, vmem_limit_bytes=56 * 1024 * 1024
        ),
        name="gather_sum_exchange",
    )(
        tokens,
        base_up_matrix.reshape(WIDTH, WIDTH),
        adapter_down_maps.reshape(128, WIDTH),
        adapter_up_maps.reshape(128, COLS),
        request_adapter.reshape(1, ROWS),
        adapter_storage.reshape(1, 64),
    )


def solution(mesh):
    return jax.shard_map(
        local,
        mesh=mesh,
        in_specs=(
            P("dp", "tensor"),
            P("tensor", "dp", None),
            P("dp", None, "tensor"),
            P("dp", None, "tensor"),
            P("dp", None),
            P(),
        ),
        out_specs=P("dp", "tensor"),
        check_vma=False,
    )
```

```python
import jax
import jax.numpy as jnp
from jax import lax
from jax.experimental import pallas as pl
from jax.experimental.pallas import tpu as pltpu
from jax.sharding import PartitionSpec as P

MESH = pl.DeviceIdType.MESH
F32 = jnp.float32
BF16 = jnp.bfloat16

NZ = 16
NDP = 32
ROWS = 64
WIDTH = 928
WPAD = 1024
SHARE = 58
SPAD = 64
CHUNKS = 4
CTOK = 512
CROWS = 240
COLS = 1856
CPAD = 1920

OFFSETS = (
    ((0, 0), (1, 0), (3, 0), (0, 1)),
    ((0, 3), (1, 1), (1, 3), (3, 1)),
    ((3, 3), (2, 0), (0, 2), (2, 1)),
    ((2, 3), (1, 2), (3, 2), (2, 2)),
)
POS = {offset: 4 * n + q for n, chunk in enumerate(OFFSETS) for q, offset in enumerate(chunk)}

PARTS = tuple(
    [(1, 0, "F"), (3, 0, "F"), (2, 0, "a"), (2, 0, "b")]
    + [(f, g, part) for f in range(4) for g, part in ((1, "F"), (3, "F"), (2, "a"), (2, "b"))]
)

ORDER = (
    "w0", "w1", "w2", "w3", "10F", "30F", "01F", "03F", "20a", "m00",
    "13F", "s00", "11F", "20b", "m01", "m02", "m03", "31F", "33F", "02a",
    "02b", "l0", "s01", "12b", "12a", "m10", "s10", "m11", "21F", "23F",
    "m12", "32a", "32b", "m13", "s02", "m20", "s20", "22a", "22b", "s11",
    "m21", "m22", "m23", "m30", "s30", "s03", "m31", "m32", "s21", "m33",
    "l1", "s12", "l2", "l3", "shrink", "s31", "s22", "s13", "s32", "s23",
    "s14", "reduce", "s33", "s24", "s04", "s34", "s25", "s15", "grow", "s35",
    "s05", "s26", "s36", "s16", "s06", "sort", "s37", "s27", "s17", "s07",
    "s38", "s28", "delta", "s18", "s08",
)


def dot_nt(a, b):
    return lax.dot_general(a, b, (((1,), (1,)), ((), ())), preferred_element_type=F32)


def dot_nn(a, b):
    return lax.dot_general(a, b, (((1,), (0,)), ((), ())), preferred_element_type=F32)


def iota(shape, dim):
    return lax.broadcasted_iota(jnp.int32, shape, dim)


def erf(x):
    x = jnp.clip(x, -4.0, 4.0)
    s = x * x
    p = -2.72614225801306e-10
    for c in (
        2.77068142495902e-08,
        -2.10102402082508e-06,
        -5.69250639462346e-05,
        -7.34990630326855e-04,
        -2.95459980854025e-03,
        -1.60960333262415e-02,
    ):
        p = p * s + c
    q = -1.45660718464996e-05
    for c in (-2.13374055278905e-04, -1.68282697438203e-03, -7.37332916720468e-03, -1.42647390514189e-02):
        q = q * s + c
    return x * p / q


def kernel(
    tok_ref, w_any, down_any, up_any, req_ref, sto_ref, out_ref,
    w_ref, down_ref, up_ref, xbuf, wt, low, ylong, yshort, first, h, lbuf, sbuf, both, total, rbuf, stack, sel,
    zsend, zrecv, zred, zgather, shrx, dbuf, ebuf, fbuf, gbuf, dterm,
    in_s, ag_s, ag_r, fw_s, fw_r, l_s, l_r, s_s, s_r, r_s, r_r,
    z1_s, z1_r, z2_s, z2_r, e_s, e_r, g_s, g_r,
):
    dp = lax.axis_index("dp")
    z = lax.axis_index("tensor")
    core = lax.rem(dp, 2)
    cy = lax.rem(dp // 2, 4)
    cx = dp // 8
    along_own = cy + core * (cx - cy)
    first_core = along_own * 2 + core
    e_slot = core * 4 + along_own
    z_own = lax.rem(cx + cy + 2 * core, 4)
    way = 1 - 2 * core

    def dev(x, yy, c):
        return (lax.rem(x, 4) * 4 + lax.rem(yy, 4)) * 2 + c

    partner = dev(cx, cy, 1 - core)

    def along_first(other):
        spot, c = other // 2, lax.rem(other, 2)
        return dev(cx + core * (spot + 4 - cx), spot + core * (cy + 4 - spot), c)

    steps = {
        ("f", 1): dev(cx + core, cy + 1 - core, core),
        ("f", 3): dev(cx + 3 * core, cy + 3 * (1 - core), core),
        ("g", 1): dev(cx + 1 - core, cy + core, core),
        ("g", 3): dev(cx + 3 * (1 - core), cy + 3 * core, core),
    }

    def remote(src, dst, ssem, rsem, target):
        return pltpu.make_async_remote_copy(
            src_ref=src, dst_ref=dst, send_sem=ssem, recv_sem=rsem, device_id=target, device_id_type=MESH
        )

    barrier = pltpu.get_barrier_semaphore()

    @pl.loop(1, NZ)
    def _(i):
        pl.semaphore_signal(barrier, inc=1, device_id=(dp, lax.rem(z + i, NZ)), device_id_type=MESH)

    @pl.loop(1, NDP)
    def _(i):
        pl.semaphore_signal(barrier, inc=1, device_id=(lax.rem(dp + i, NDP), z), device_id_type=MESH)

    loads = {
        "w": pltpu.make_async_copy(w_any, w_ref, in_s.at[0]),
        "down": pltpu.make_async_copy(down_any, down_ref, in_s.at[1]),
        "up": pltpu.make_async_copy(up_any, up_ref, in_s.at[2]),
    }
    for load in loads.values():
        load.start()

    diagonal = iota((ROWS, ROWS), 0) == iota((ROWS, ROWS), 1)
    adapter = jnp.sum(jnp.where(diagonal, req_ref[...], 0), axis=1, keepdims=True)
    onehot = adapter == iota((ROWS, 64), 1)
    slot = jnp.sum(jnp.where(onehot, sto_ref[...], 0), axis=1, keepdims=True)
    lower = (iota((ROWS, ROWS), 1) < iota((ROWS, ROWS), 0)).astype(F32).astype(BF16)
    before = dot_nn(lower, onehot.astype(F32).astype(BF16))
    rank = jnp.sum(jnp.where(onehot, before, 0.0), axis=1, keepdims=True)
    place = slot.astype(F32) * 2.0 + rank
    xbuf[0, core, :, WPAD - 128 : WPAD] = jnp.broadcast_to(place, (ROWS, 128)).astype(BF16)
    xbuf[0, core, :, 0:WIDTH] = tok_ref[...]

    pl.semaphore_wait(barrier, NDP - 1 + NZ - 1)

    def where_at(f, g):
        return POS[g, f] + core * (POS[f, g] - POS[g, f])

    def part_copy(f, g, part):
        axis, d = ("f", f) if g == 0 else ("g", g)
        if part == "F":
            start, size, back, way_on = 0, ROWS, d, d
        else:
            start, size = (0, ROWS // 2) if part == "a" else (ROWS // 2, ROWS // 2)
            back = way_on = 1 if part == "a" else 3
        if part == "F":
            source = (0, 0) if g == 0 else (f, 0)
        else:
            source = (back, 0) if g == 0 else (f, back)
        i = PARTS.index((f, g, part))
        rows = pl.ds(start, size)
        return remote(
            xbuf.at[where_at(*source), core, rows], xbuf.at[where_at(f, g), core, rows],
            ag_s.at[i], ag_r.at[i], (steps[axis, way_on], z),
        )

    def forward(p):
        return remote(xbuf.at[p, core], xbuf.at[p, core], fw_s.at[p], fw_r.at[p], (partner, z))

    for part in ((1, 0, "F"), (3, 0, "F"), (0, 1, "F"), (0, 3, "F")):
        part_copy(*part).start()
    forward(0).start()

    low[...] = jnp.zeros_like(low)
    dbuf[...] = jnp.zeros_like(dbuf)
    ylong[:, :, CROWS - 8 : CROWS] = jnp.zeros((CHUNKS, 8, 8, 128), F32)
    yshort[:, :, CROWS - 8 : CROWS] = jnp.zeros((CHUNKS, 8, 8, 128), F32)

    arrived = {}

    def gathered(f, g, part):
        part_copy(f, g, part).wait_recv()
        if part == "F":
            half = "a" if (f if g == 0 else g) == 1 else "b"
            part_copy(2, 0, half).start() if g == 0 else part_copy(f, 2, half).start()
        else:
            arrived[f, g] = arrived.get((f, g), 0) + 1
            if arrived[f, g] < 2:
                return
        forward(where_at(f, g)).start()
        if g == 0:
            part_copy(f, 1, "F").start()
            part_copy(f, 3, "F").start()

    def offsets(b):
        return (8 - 2 * b, 9 + 2 * b, 7 - 2 * b, 10 + 2 * b)

    def weights(b):
        if b == 0:
            loads["w"].wait()
        row = iota((256, WIDTH), 0)
        plane = jnp.zeros((256, WIDTH), jnp.int32)
        for j, o in enumerate(offsets(b)):
            plane = jnp.where(row // SPAD == j, lax.rem(z + way * o + NZ, NZ), plane)
        unit = plane * SHARE + row % SPAD
        pickrow = jnp.where((row % SPAD < SHARE) & (unit == iota((256, WIDTH), 1)), 1.0, 0.0).astype(BF16)
        wt[b, :, WPAD - 128 : WPAD] = jnp.zeros((256, 128), BF16)
        wt[b, :, 0:WIDTH] = dot_nt(pickrow, w_ref[...]).astype(BF16)
        if b == 3:
            loads["down"].wait()
            low[:, 0:WIDTH] = down_ref[...]

    def multiply(n, b):
        if b == 0:
            for q in range(4):
                p = 4 * n + q
                remote(xbuf.at[p, 1 - core], xbuf.at[p, 1 - core], fw_s.at[p], fw_r.at[p], (partner, z)).wait_recv()
        x = xbuf[4 * n : 4 * n + 4].reshape(CTOK, WPAD)
        part = dot_nt(wt[b], x)
        for j in range(4):
            dest, s = (ylong, yshort)[j % 2], 2 * b + j // 2
            for q in range(4):
                dest[n, s, q * SHARE : (q + 1) * SHARE] = part[j * SPAD : j * SPAD + SHARE, q * 128 : (q + 1) * 128]

    def down(n):
        x = xbuf[4 * n : 4 * n + 4].reshape(CTOK, WPAD)
        part = dot_nt(low[...], x).astype(BF16)
        for q in range(4):
            h[4 * n + q] = part[:, q * 128 : (q + 1) * 128]

    def long_hop(n, s, src):
        return remote(src, lbuf.at[n, s], l_s.at[n, s], l_r.at[n, s], (dp, lax.rem(z + way + NZ, NZ)))

    def short_hop(n, s, src):
        return remote(src, sbuf.at[n, s], s_s.at[n, s], s_r.at[n, s], (dp, lax.rem(z - way + NZ, NZ)))

    def result(n, q, c):
        dx, dy = OFFSETS[n][q]
        target = dev(cx + 4 - dx, cy + 4 - dy, c)
        return remote(total.at[n, q, c], rbuf.at[dp], r_s.at[n, q, c], r_r.at[n, q, core], (target, z))

    def result_arrives(n, q, c):
        dx, dy = OFFSETS[n][q]
        source = dev(cx + dx, cy + dy, c)
        return remote(total.at[n, q, c], rbuf.at[source], r_s.at[n, q, c], r_r.at[n, q, c], (partner, z))

    def others(n, q, c, what):
        if n == 0 and q == 0:

            @pl.when(core != c)
            def _():
                what(n, q, c)

        else:
            what(n, q, c)

    left = iota((32, 128), 1) < 64

    def stage(n, s):
        if s == 0:
            first[n, 0] = ylong[n, 0].astype(BF16)
            long_hop(n, 0, first.at[n, 0]).start()
            first[n, 1] = yshort[n, 0].astype(BF16)
            short_hop(n, 0, first.at[n, 1]).start()
        if 1 <= s <= 7:
            here = lbuf.at[n, s - 1]
            long_hop(n, s - 1, here).wait_recv()
            lbuf[n, s - 1] = (lbuf[n, s - 1].astype(F32) + ylong[n, s]).astype(BF16)
            long_hop(n, s, here).start()
        if 1 <= s <= 6:
            here = sbuf.at[n, s - 1]
            short_hop(n, s - 1, here).wait_recv()
            sbuf[n, s - 1] = (sbuf[n, s - 1].astype(F32) + yshort[n, s]).astype(BF16)
            short_hop(n, s, here).start()
        if s == 8:
            short_hop(n, 6, sbuf.at[n, 6]).wait_recv()
            long_hop(n, 7, lbuf.at[n, 7]).wait_recv()
            both[...] = lbuf[n, 7].astype(F32) + sbuf[n, 6].astype(F32) + yshort[n, 7]
            for q in range(4):
                upper = both[q * SHARE : q * SHARE + 32]
                under = both[q * SHARE + 32 : q * SHARE + 64]
                total[n, q, 0] = jnp.where(left, upper, pltpu.roll(under, 64, 1)).astype(BF16)
                total[n, q, 1] = jnp.where(left, pltpu.roll(upper, 64, 1), under).astype(BF16)
                for c in range(2):
                    others(n, q, c, lambda *a: result(*a).start())
            if n == 0:
                rbuf[dp] = total[0, 0, core]

    lane64 = iota((64, 128), 1)

    def shrink():
        key = dp * 4
        for n in range(CHUNKS):
            for q in range(4):
                p = 4 * n + q
                dx, dy = OFFSETS[n][q]
                x = lax.rem(cx + 4 - dx, 4)
                yy = lax.rem(cy + 4 - dy, 4)
                along, across = yy + core * (x - yy), x + core * (yy - x)
                meta = dot_nt(
                    jnp.where(iota((16, 128), 1) == 127, 1.0, 0.0).astype(BF16),
                    xbuf[p, :, :, WPAD - 128 : WPAD].reshape(128, 128),
                )[0:1]
                row = iota((128, 128), 0)
                home = (along * 2 + iota((128, 128), 1) // 64) * 4 + across
                wanted = key + 2 * (row // 64) + row % 2
                hit = ((row % 64) // 2 == home) & (meta.astype(jnp.int32) == wanted)
                sel[p] = jnp.where(hit, 1.0, 0.0).astype(BF16)
        acc = jnp.zeros((128, 128), F32)
        for p in range(16):
            acc = acc + dot_nt(sel[p], h[p])
        part = jnp.where(lane64 < 64, acc[0:64], acc[64:128]).astype(BF16)
        for q in range(4):
            zsend[q] = part[16 * q : 16 * q + 16]
            owner = 4 * q + z_own

            @pl.when(owner != z)
            def _():
                remote(zsend.at[q], zrecv.at[z], z1_s.at[q], z1_r.at[z], (dp, owner)).start()

            @pl.when(owner == z)
            def _():
                zrecv[z] = zsend[q]

    def reduce():
        @pl.when(lax.rem(z, 4) == z_own)
        def _():
            @pl.loop(1, NZ)
            def _(i):
                other = lax.rem(z + i, NZ)
                remote(zsend.at[0], zrecv.at[other], z1_s.at[0], z1_r.at[other], (dp, other)).wait_recv()

            whole = zrecv[0].astype(F32)
            for i in range(1, NZ):
                whole = whole + zrecv[i].astype(F32)
            zred[...] = whole.astype(BF16)

            @pl.loop(1, NZ)
            def _(i):
                other = lax.rem(z + i, NZ)
                remote(zred, zgather.at[z // 4], z2_s.at[i], z2_r.at[z // 4], (dp, other)).start()

            zgather[z // 4] = zred[...]

    def grow():
        for q in range(4):

            @pl.when(4 * q + z_own != z)
            def _():
                remote(zred, zgather.at[q], z2_s.at[1], z2_r.at[q], (dp, 4 * q + z_own)).wait_recv()

        rows = zgather[...].reshape(64, 128).astype(F32)
        for g in range(8):
            eight = rows[8 * g : 8 * g + 8]
            lane = lane64[0:8]
            shrx[16 * g : 16 * g + 8] = jnp.where(lane < 64, eight, 0.0)
            shrx[16 * g + 8 : 16 * g + 16] = jnp.where(lane < 64, 0.0, eight)
        loads["up"].wait()
        grown = dot_nn(shrx[...].astype(BF16), up_ref[...])
        dbuf[:, :, 0:COLS] = grown.reshape(8, 16, COLS).astype(BF16)

        @pl.loop(1, 8)
        def _(i):
            other = lax.rem(first_core + i, 8)
            remote(dbuf.at[other], ebuf.at[e_slot], e_s.at[i], e_r.at[e_slot], (along_first(other), z)).start()

        ebuf[e_slot] = dbuf[first_core]

    def sort():
        @pl.loop(1, 8)
        def _(i):
            slot = lax.rem(e_slot + i, 8)
            remote(dbuf.at[slot], ebuf.at[slot], e_s.at[i], e_r.at[slot], (partner, z)).wait_recv()

        to = iota((128, 128), 0)
        place_of = to // 16
        origin = (place_of // 4) * 4 + (to // 4) % 4
        source = origin * 16 + ((to // 2) % 2) * 8 + (place_of % 4) * 2 + to % 2
        perm = jnp.where(iota((128, 128), 1) == source, 1.0, 0.0).astype(BF16)
        fbuf[...] = dot_nn(perm, ebuf[...].reshape(128, CPAD)).reshape(8, 16, CPAD).astype(BF16)

        @pl.loop(1, 4)
        def _(i):
            to_x, to_y = lax.rem(cx + i, 4), lax.rem(cy + i, 4)
            remote(fbuf.at[to_x], gbuf.at[cx], g_s.at[i], g_r.at[i], (dev(to_x, cy, core), z)).start()
            remote(fbuf.at[4 + to_y], gbuf.at[4 + cy], g_s.at[4 + i], g_r.at[4 + i], (dev(cx, to_y, core), z)).start()

        gbuf[cx] = fbuf[cx]
        gbuf[4 + cy] = fbuf[4 + cy]

    def deltas():
        @pl.loop(1, 4)
        def _(i):
            of_x, of_y = lax.rem(cx + 4 - i, 4), lax.rem(cy + 4 - i, 4)
            remote(fbuf.at[0], gbuf.at[of_x], g_s.at[i], g_r.at[i], (partner, z)).wait_recv()
            remote(fbuf.at[0], gbuf.at[4 + of_y], g_s.at[4 + i], g_r.at[4 + i], (partner, z)).wait_recv()

        lane = iota((ROWS, 128), 1)
        line, step = lane // 16, (lane // 4) % 4
        owner = jnp.where(line < 4, (line * 4 + step) * 2, (step * 4 + line - 4) * 2 + 1)
        mine = (place.astype(jnp.int32) == owner * 4 + lane % 4).astype(F32).astype(BF16)
        dterm[...] = dot_nn(mine, gbuf[...].reshape(128, CPAD))[:, 0:COLS]

    adapters = {"shrink": shrink, "reduce": reduce, "grow": grow, "sort": sort, "delta": deltas}
    for word in ORDER:
        if word in adapters:
            adapters[word]()
        elif word[0] == "w":
            weights(int(word[1]))
        elif word[0] == "m":
            multiply(int(word[1]), int(word[2]))
        elif word[0] == "s":
            stage(int(word[1]), int(word[2]))
        elif word[0] == "l":
            down(int(word[1]))
        else:
            gathered(int(word[0]), int(word[1]), word[2])

    for part in PARTS:
        if part != (0, 0, "F"):
            part_copy(*part).wait_send()
    for p in range(16):
        forward(p).wait_send()
    for n in range(CHUNKS):
        for s in range(8):
            long_hop(n, s, lbuf.at[n, s]).wait_send()
        for s in range(7):
            short_hop(n, s, sbuf.at[n, s]).wait_send()

    for q in range(4):

        @pl.when(4 * q + z_own != z)
        def _():
            remote(zsend.at[q], zrecv.at[z], z1_s.at[q], z1_r.at[z], (partner, z)).wait_send()

    @pl.when(lax.rem(z, 4) == z_own)
    def _():
        @pl.loop(1, NZ)
        def _(i):
            remote(zred, zgather.at[0], z2_s.at[i], z2_r.at[0], (partner, z)).wait_send()

    @pl.loop(1, 8)
    def _(i):
        remote(dbuf.at[i], ebuf.at[i], e_s.at[i], e_r.at[i], (partner, z)).wait_send()

    @pl.loop(1, 4)
    def _(i):
        remote(fbuf.at[0], gbuf.at[0], g_s.at[i], g_r.at[i], (partner, z)).wait_send()
        remote(fbuf.at[0], gbuf.at[0], g_s.at[4 + i], g_r.at[4 + i], (partner, z)).wait_send()

    for n in range(CHUNKS):
        for q in range(4):
            for c in range(2):
                others(n, q, c, lambda *a: result(*a).wait_send())
    for n in range(CHUNKS):
        for q in range(4):
            for c in range(2):
                others(n, q, c, lambda *a: result_arrives(*a).wait_recv())

    for k in range(NDP):
        got = rbuf[k].astype(F32)
        stack[k * SHARE : k * SHARE + 32] = jnp.where(left, got, 0.0)
        stack[k * SHARE + 32 : (k + 1) * SHARE] = jnp.where(left, 0.0, got)[0 : SHARE - 32]
    turn = jnp.where(iota((ROWS, 128), 1) % 64 == iota((ROWS, 128), 0), 1.0, 0.0).astype(BF16)
    v = dot_nt(turn, stack[...].astype(BF16)) + dterm[...]
    out_ref[...] = (0.5 * v * (1.0 + erf(v * 0.7071067811865476))).astype(BF16)


def local(tokens, base_up_matrix, adapter_down_maps, adapter_up_maps, request_adapter, adapter_storage):
    dma = pltpu.SemaphoreType.DMA
    vmem = pl.BlockSpec(memory_space=pltpu.VMEM)
    hbm = pl.BlockSpec(memory_space=pl.ANY)
    return pl.pallas_call(
        kernel,
        out_shape=jax.ShapeDtypeStruct((ROWS, COLS), BF16),
        in_specs=[vmem, hbm, hbm, hbm, vmem, vmem],
        out_specs=vmem,
        scratch_shapes=[
            pltpu.VMEM((WIDTH, WIDTH), BF16),
            pltpu.VMEM((128, WIDTH), BF16),
            pltpu.VMEM((128, COLS), BF16),
            pltpu.VMEM((16, 2, ROWS, WPAD), BF16),
            pltpu.VMEM((4, 256, WPAD), BF16),
            pltpu.VMEM((128, WPAD), BF16),
            pltpu.VMEM((CHUNKS, 8, CROWS, 128), F32),
            pltpu.VMEM((CHUNKS, 8, CROWS, 128), F32),
            pltpu.VMEM((CHUNKS, 2, CROWS, 128), BF16),
            pltpu.VMEM((16, 128, 128), BF16),
            pltpu.VMEM((CHUNKS, 8, CROWS, 128), BF16),
            pltpu.VMEM((CHUNKS, 7, CROWS, 128), BF16),
            pltpu.VMEM((CROWS, 128), F32),
            pltpu.VMEM((CHUNKS, 4, 2, 32, 128), BF16),
            pltpu.VMEM((NDP, 32, 128), BF16),
            pltpu.VMEM((COLS, 128), F32),
            pltpu.VMEM((16, 128, 128), BF16),
            pltpu.VMEM((4, 16, 128), BF16),
            pltpu.VMEM((NZ, 16, 128), BF16),
            pltpu.VMEM((16, 128), BF16),
            pltpu.VMEM((4, 16, 128), BF16),
            pltpu.VMEM((128, 128), F32),
            pltpu.VMEM((8, 16, CPAD), BF16),
            pltpu.VMEM((8, 16, CPAD), BF16),
            pltpu.VMEM((8, 16, CPAD), BF16),
            pltpu.VMEM((8, 16, CPAD), BF16),
            pltpu.VMEM((ROWS, COLS), F32),
            dma((3,)), dma((len(PARTS),)), dma((len(PARTS),)), dma((16,)), dma((16,)),
            dma((CHUNKS, 8)), dma((CHUNKS, 8)), dma((CHUNKS, 7)), dma((CHUNKS, 7)),
            dma((CHUNKS, 4, 2)), dma((CHUNKS, 4, 2)),
            dma((4,)), dma((NZ,)), dma((NZ,)), dma((4,)),
            dma((8,)), dma((8,)), dma((8,)), dma((8,)),
        ],
        compiler_params=pltpu.CompilerParams(
            collective_id=0, has_side_effects=True, vmem_limit_bytes=56 * 1024 * 1024
        ),
        name="gather_sum_exchange",
    )(
        tokens,
        base_up_matrix.reshape(WIDTH, WIDTH),
        adapter_down_maps.reshape(128, WIDTH),
        adapter_up_maps.reshape(128, COLS),
        request_adapter.reshape(1, ROWS),
        adapter_storage.reshape(1, 64),
    )


def solution(mesh):
    return jax.shard_map(
        local,
        mesh=mesh,
        in_specs=(
            P("dp", "tensor"),
            P("tensor", "dp", None),
            P("dp", None, "tensor"),
            P("dp", None, "tensor"),
            P("dp", None),
            P(),
        ),
        out_specs=P("dp", "tensor"),
        check_vma=False,
    )
```

```python
import jax
import jax.numpy as jnp
from jax import lax
from jax.experimental import pallas as pl
from jax.experimental.pallas import tpu as pltpu
from jax.sharding import PartitionSpec as P

MESH = pl.DeviceIdType.MESH
F32 = jnp.float32
BF16 = jnp.bfloat16

NZ = 16
NDP = 32
ROWS = 64
WIDTH = 928
WPAD = 1024
SHARE = 58
SPAD = 64
CHUNKS = 4
CTOK = 512
CROWS = 240
COLS = 1856
CPAD = 1920

OFFSETS = (
    ((0, 0), (1, 0), (3, 0), (0, 1)),
    ((0, 3), (1, 1), (1, 3), (3, 1)),
    ((3, 3), (2, 0), (0, 2), (2, 1)),
    ((2, 3), (1, 2), (3, 2), (2, 2)),
)
POS = {offset: 4 * n + q for n, chunk in enumerate(OFFSETS) for q, offset in enumerate(chunk)}

PARTS = tuple(
    [(1, 0, "F"), (3, 0, "F"), (2, 0, "a"), (2, 0, "b")]
    + [(f, g, part) for f in range(4) for g, part in ((1, "F"), (3, "F"), (2, "a"), (2, "b"))]
)

ORDER = (
    "w0", "w1", "w2", "w3", "10F", "30F", "01F", "03F", "20a", "m00",
    "13F", "r1", "s00", "11F", "20b", "m01", "m02", "m03", "r2", "31F",
    "33F", "02a", "02b", "l0", "s01", "r3", "12b", "12a", "m10", "s10",
    "m11", "21F", "r4", "23F", "m12", "32a", "32b", "m13", "s02", "m20",
    "r5", "s20", "22a", "22b", "s11", "m21", "m22", "r6", "m23", "m30",
    "s30", "s03", "m31", "m32", "r7", "s21", "m33", "l1", "s12", "l2",
    "l3", "r8", "shrink", "s31", "s22", "s13", "s32", "s23", "s14", "reduce",
    "s33", "s24", "s04", "s34", "s25", "s15", "grow", "s35", "s05", "s26",
    "s36", "s16", "s06", "sort", "s37", "s27", "s17", "s07", "s38", "s28",
    "delta", "s18", "s08",
)


def dot_nt(a, b):
    return lax.dot_general(a, b, (((1,), (1,)), ((), ())), preferred_element_type=F32)


def dot_nn(a, b):
    return lax.dot_general(a, b, (((1,), (0,)), ((), ())), preferred_element_type=F32)


def iota(shape, dim):
    return lax.broadcasted_iota(jnp.int32, shape, dim)


def erf(x):
    x = jnp.clip(x, -4.0, 4.0)
    s = x * x
    p = -2.72614225801306e-10
    for c in (
        2.77068142495902e-08,
        -2.10102402082508e-06,
        -5.69250639462346e-05,
        -7.34990630326855e-04,
        -2.95459980854025e-03,
        -1.60960333262415e-02,
    ):
        p = p * s + c
    q = -1.45660718464996e-05
    for c in (-2.13374055278905e-04, -1.68282697438203e-03, -7.37332916720468e-03, -1.42647390514189e-02):
        q = q * s + c
    return x * p / q


def kernel(
    tok_ref, w_any, down_any, up_any, req_ref, sto_ref, out_ref,
    w_ref, down_ref, up_ref, xbuf, wt, low, ylong, yshort, first, h, lbuf, sbuf, both, total, rbuf, stack, sel,
    zsend, zrecv, zred, zgather, shrx, dbuf, ebuf, fbuf, gbuf, dterm,
    in_s, ag_s, ag_r, fw_s, fw_r, l_s, l_r, s_s, s_r, r_s, r_r,
    z1_s, z1_r, z2_s, z2_r, e_s, e_r, g_s, g_r, ring,
):
    dp = lax.axis_index("dp")
    z = lax.axis_index("tensor")
    core = lax.rem(dp, 2)
    cy = lax.rem(dp // 2, 4)
    cx = dp // 8
    along_own = cy + core * (cx - cy)
    first_core = along_own * 2 + core
    e_slot = core * 4 + along_own
    z_own = lax.rem(cx + cy + 2 * core, 4)
    way = 1 - 2 * core

    def dev(x, yy, c):
        return (lax.rem(x, 4) * 4 + lax.rem(yy, 4)) * 2 + c

    partner = dev(cx, cy, 1 - core)

    def along_first(other):
        spot, c = other // 2, lax.rem(other, 2)
        return dev(cx + core * (spot + 4 - cx), spot + core * (cy + 4 - spot), c)

    steps = {
        ("f", 1): dev(cx + core, cy + 1 - core, core),
        ("f", 3): dev(cx + 3 * core, cy + 3 * (1 - core), core),
        ("g", 1): dev(cx + 1 - core, cy + core, core),
        ("g", 3): dev(cx + 3 * (1 - core), cy + 3 * core, core),
    }

    def remote(src, dst, ssem, rsem, target):
        return pltpu.make_async_remote_copy(
            src_ref=src, dst_ref=dst, send_sem=ssem, recv_sem=rsem, device_id=target, device_id_type=MESH
        )

    barrier = pltpu.get_barrier_semaphore()
    above, below = (dp, lax.rem(z + 1, NZ)), (dp, lax.rem(z + NZ - 1, NZ))
    near = [(dev(cx + 1, cy, core), z), (dev(cx + 3, cy, core), z), (dev(cx, cy + 1, core), z)]
    near += [(dev(cx, cy + 3, core), z), (partner, z), above, below]
    for device in near:
        pl.semaphore_signal(barrier, inc=1, device_id=device, device_id_type=MESH)

    loads = {
        "w": pltpu.make_async_copy(w_any, w_ref, in_s.at[0]),
        "down": pltpu.make_async_copy(down_any, down_ref, in_s.at[1]),
        "up": pltpu.make_async_copy(up_any, up_ref, in_s.at[2]),
    }
    for load in loads.values():
        load.start()

    diagonal = iota((ROWS, ROWS), 0) == iota((ROWS, ROWS), 1)
    adapter = jnp.sum(jnp.where(diagonal, req_ref[...], 0), axis=1, keepdims=True)
    onehot = adapter == iota((ROWS, 64), 1)
    slot = jnp.sum(jnp.where(onehot, sto_ref[...], 0), axis=1, keepdims=True)
    lower = (iota((ROWS, ROWS), 1) < iota((ROWS, ROWS), 0)).astype(F32).astype(BF16)
    before = dot_nn(lower, onehot.astype(F32).astype(BF16))
    rank = jnp.sum(jnp.where(onehot, before, 0.0), axis=1, keepdims=True)
    place = slot.astype(F32) * 2.0 + rank
    xbuf[0, core, :, WPAD - 128 : WPAD] = jnp.broadcast_to(place, (ROWS, 128)).astype(BF16)
    xbuf[0, core, :, 0:WIDTH] = tok_ref[...]

    pl.semaphore_wait(barrier, len(near))

    def greet(k):
        if k > 0:
            pl.semaphore_wait(ring.at[0], 1)
            pl.semaphore_wait(ring.at[1], 1)
        if k < 8:
            pl.semaphore_signal(ring.at[0], inc=1, device_id=above, device_id_type=MESH)
            pl.semaphore_signal(ring.at[1], inc=1, device_id=below, device_id_type=MESH)

    greet(0)

    def where_at(f, g):
        return POS[g, f] + core * (POS[f, g] - POS[g, f])

    def part_copy(f, g, part):
        axis, d = ("f", f) if g == 0 else ("g", g)
        if part == "F":
            start, size, back, way_on = 0, ROWS, d, d
        else:
            start, size = (0, ROWS // 2) if part == "a" else (ROWS // 2, ROWS // 2)
            back = way_on = 1 if part == "a" else 3
        if part == "F":
            source = (0, 0) if g == 0 else (f, 0)
        else:
            source = (back, 0) if g == 0 else (f, back)
        i = PARTS.index((f, g, part))
        rows = pl.ds(start, size)
        return remote(
            xbuf.at[where_at(*source), core, rows], xbuf.at[where_at(f, g), core, rows],
            ag_s.at[i], ag_r.at[i], (steps[axis, way_on], z),
        )

    def forward(p):
        return remote(xbuf.at[p, core], xbuf.at[p, core], fw_s.at[p], fw_r.at[p], (partner, z))

    for part in ((1, 0, "F"), (3, 0, "F"), (0, 1, "F"), (0, 3, "F")):
        part_copy(*part).start()
    forward(0).start()

    low[...] = jnp.zeros_like(low)
    dbuf[...] = jnp.zeros_like(dbuf)
    ylong[:, :, CROWS - 8 : CROWS] = jnp.zeros((CHUNKS, 8, 8, 128), F32)
    yshort[:, :, CROWS - 8 : CROWS] = jnp.zeros((CHUNKS, 8, 8, 128), F32)

    arrived = {}

    def gathered(f, g, part):
        part_copy(f, g, part).wait_recv()
        if part == "F":
            half = "a" if (f if g == 0 else g) == 1 else "b"
            part_copy(2, 0, half).start() if g == 0 else part_copy(f, 2, half).start()
        else:
            arrived[f, g] = arrived.get((f, g), 0) + 1
            if arrived[f, g] < 2:
                return
        forward(where_at(f, g)).start()
        if g == 0:
            part_copy(f, 1, "F").start()
            part_copy(f, 3, "F").start()

    def offsets(b):
        return (8 - 2 * b, 9 + 2 * b, 7 - 2 * b, 10 + 2 * b)

    def weights(b):
        if b == 0:
            loads["w"].wait()
        row = iota((256, WIDTH), 0)
        plane = jnp.zeros((256, WIDTH), jnp.int32)
        for j, o in enumerate(offsets(b)):
            plane = jnp.where(row // SPAD == j, lax.rem(z + way * o + NZ, NZ), plane)
        unit = plane * SHARE + row % SPAD
        pickrow = jnp.where((row % SPAD < SHARE) & (unit == iota((256, WIDTH), 1)), 1.0, 0.0).astype(BF16)
        wt[b, :, WPAD - 128 : WPAD] = jnp.zeros((256, 128), BF16)
        wt[b, :, 0:WIDTH] = dot_nt(pickrow, w_ref[...]).astype(BF16)
        if b == 3:
            loads["down"].wait()
            low[:, 0:WIDTH] = down_ref[...]

    def multiply(n, b):
        if b == 0:
            for q in range(4):
                p = 4 * n + q
                remote(xbuf.at[p, 1 - core], xbuf.at[p, 1 - core], fw_s.at[p], fw_r.at[p], (partner, z)).wait_recv()
        x = xbuf[4 * n : 4 * n + 4].reshape(CTOK, WPAD)
        part = dot_nt(wt[b], x)
        for j in range(4):
            dest, s = (ylong, yshort)[j % 2], 2 * b + j // 2
            for q in range(4):
                dest[n, s, q * SHARE : (q + 1) * SHARE] = part[j * SPAD : j * SPAD + SHARE, q * 128 : (q + 1) * 128]

    def down(n):
        x = xbuf[4 * n : 4 * n + 4].reshape(CTOK, WPAD)
        part = dot_nt(low[...], x).astype(BF16)
        for q in range(4):
            h[4 * n + q] = part[:, q * 128 : (q + 1) * 128]

    def long_hop(n, s, src):
        return remote(src, lbuf.at[n, s], l_s.at[n, s], l_r.at[n, s], (dp, lax.rem(z + way + NZ, NZ)))

    def short_hop(n, s, src):
        return remote(src, sbuf.at[n, s], s_s.at[n, s], s_r.at[n, s], (dp, lax.rem(z - way + NZ, NZ)))

    def result(n, q, c):
        dx, dy = OFFSETS[n][q]
        target = dev(cx + 4 - dx, cy + 4 - dy, c)
        return remote(total.at[n, q, c], rbuf.at[dp], r_s.at[n, q, c], r_r.at[n, q, core], (target, z))

    def result_arrives(n, q, c):
        dx, dy = OFFSETS[n][q]
        source = dev(cx + dx, cy + dy, c)
        return remote(total.at[n, q, c], rbuf.at[source], r_s.at[n, q, c], r_r.at[n, q, c], (partner, z))

    def others(n, q, c, what):
        if n == 0 and q == 0:

            @pl.when(core != c)
            def _():
                what(n, q, c)

        else:
            what(n, q, c)

    left = iota((32, 128), 1) < 64

    def stage(n, s):
        if s == 0:
            first[n, 0] = ylong[n, 0].astype(BF16)
            long_hop(n, 0, first.at[n, 0]).start()
            first[n, 1] = yshort[n, 0].astype(BF16)
            short_hop(n, 0, first.at[n, 1]).start()
        if 1 <= s <= 7:
            here = lbuf.at[n, s - 1]
            long_hop(n, s - 1, here).wait_recv()
            lbuf[n, s - 1] = (lbuf[n, s - 1].astype(F32) + ylong[n, s]).astype(BF16)
            long_hop(n, s, here).start()
        if 1 <= s <= 6:
            here = sbuf.at[n, s - 1]
            short_hop(n, s - 1, here).wait_recv()
            sbuf[n, s - 1] = (sbuf[n, s - 1].astype(F32) + yshort[n, s]).astype(BF16)
            short_hop(n, s, here).start()
        if s == 8:
            short_hop(n, 6, sbuf.at[n, 6]).wait_recv()
            long_hop(n, 7, lbuf.at[n, 7]).wait_recv()
            both[...] = lbuf[n, 7].astype(F32) + sbuf[n, 6].astype(F32) + yshort[n, 7]
            for q in range(4):
                upper = both[q * SHARE : q * SHARE + 32]
                under = both[q * SHARE + 32 : q * SHARE + 64]
                total[n, q, 0] = jnp.where(left, upper, pltpu.roll(under, 64, 1)).astype(BF16)
                total[n, q, 1] = jnp.where(left, pltpu.roll(upper, 64, 1), under).astype(BF16)
                for c in range(2):
                    others(n, q, c, lambda *a: result(*a).start())
            if n == 0:
                rbuf[dp] = total[0, 0, core]

    lane64 = iota((64, 128), 1)

    def shrink():
        key = dp * 4
        for n in range(CHUNKS):
            for q in range(4):
                p = 4 * n + q
                dx, dy = OFFSETS[n][q]
                x = lax.rem(cx + 4 - dx, 4)
                yy = lax.rem(cy + 4 - dy, 4)
                along, across = yy + core * (x - yy), x + core * (yy - x)
                meta = dot_nt(
                    jnp.where(iota((16, 128), 1) == 127, 1.0, 0.0).astype(BF16),
                    xbuf[p, :, :, WPAD - 128 : WPAD].reshape(128, 128),
                )[0:1]
                row = iota((128, 128), 0)
                home = (along * 2 + iota((128, 128), 1) // 64) * 4 + across
                wanted = key + 2 * (row // 64) + row % 2
                hit = ((row % 64) // 2 == home) & (meta.astype(jnp.int32) == wanted)
                sel[p] = jnp.where(hit, 1.0, 0.0).astype(BF16)
        acc = jnp.zeros((128, 128), F32)
        for p in range(16):
            acc = acc + dot_nt(sel[p], h[p])
        part = jnp.where(lane64 < 64, acc[0:64], acc[64:128]).astype(BF16)
        for q in range(4):
            zsend[q] = part[16 * q : 16 * q + 16]
            owner = 4 * q + z_own

            @pl.when(owner != z)
            def _():
                remote(zsend.at[q], zrecv.at[z], z1_s.at[q], z1_r.at[z], (dp, owner)).start()

            @pl.when(owner == z)
            def _():
                zrecv[z] = zsend[q]

    def reduce():
        @pl.when(lax.rem(z, 4) == z_own)
        def _():
            @pl.loop(1, NZ)
            def _(i):
                other = lax.rem(z + i, NZ)
                remote(zsend.at[0], zrecv.at[other], z1_s.at[0], z1_r.at[other], (dp, other)).wait_recv()

            whole = zrecv[0].astype(F32)
            for i in range(1, NZ):
                whole = whole + zrecv[i].astype(F32)
            zred[...] = whole.astype(BF16)

            @pl.loop(1, NZ)
            def _(i):
                other = lax.rem(z + i, NZ)
                remote(zred, zgather.at[z // 4], z2_s.at[i], z2_r.at[z // 4], (dp, other)).start()

            zgather[z // 4] = zred[...]

    def grow():
        for q in range(4):

            @pl.when(4 * q + z_own != z)
            def _():
                remote(zred, zgather.at[q], z2_s.at[1], z2_r.at[q], (dp, 4 * q + z_own)).wait_recv()

        rows = zgather[...].reshape(64, 128).astype(F32)
        for g in range(8):
            eight = rows[8 * g : 8 * g + 8]
            lane = lane64[0:8]
            shrx[16 * g : 16 * g + 8] = jnp.where(lane < 64, eight, 0.0)
            shrx[16 * g + 8 : 16 * g + 16] = jnp.where(lane < 64, 0.0, eight)
        loads["up"].wait()
        grown = dot_nn(shrx[...].astype(BF16), up_ref[...])
        dbuf[:, :, 0:COLS] = grown.reshape(8, 16, COLS).astype(BF16)

        @pl.loop(1, 8)
        def _(i):
            other = lax.rem(first_core + i, 8)
            remote(dbuf.at[other], ebuf.at[e_slot], e_s.at[i], e_r.at[e_slot], (along_first(other), z)).start()

        ebuf[e_slot] = dbuf[first_core]

    def sort():
        @pl.loop(1, 8)
        def _(i):
            slot = lax.rem(e_slot + i, 8)
            remote(dbuf.at[slot], ebuf.at[slot], e_s.at[i], e_r.at[slot], (partner, z)).wait_recv()

        to = iota((128, 128), 0)
        place_of = to // 16
        origin = (place_of // 4) * 4 + (to // 4) % 4
        source = origin * 16 + ((to // 2) % 2) * 8 + (place_of % 4) * 2 + to % 2
        perm = jnp.where(iota((128, 128), 1) == source, 1.0, 0.0).astype(BF16)
        fbuf[...] = dot_nn(perm, ebuf[...].reshape(128, CPAD)).reshape(8, 16, CPAD).astype(BF16)

        @pl.loop(1, 4)
        def _(i):
            to_x, to_y = lax.rem(cx + i, 4), lax.rem(cy + i, 4)
            remote(fbuf.at[to_x], gbuf.at[cx], g_s.at[i], g_r.at[i], (dev(to_x, cy, core), z)).start()
            remote(fbuf.at[4 + to_y], gbuf.at[4 + cy], g_s.at[4 + i], g_r.at[4 + i], (dev(cx, to_y, core), z)).start()

        gbuf[cx] = fbuf[cx]
        gbuf[4 + cy] = fbuf[4 + cy]

    def deltas():
        @pl.loop(1, 4)
        def _(i):
            of_x, of_y = lax.rem(cx + 4 - i, 4), lax.rem(cy + 4 - i, 4)
            remote(fbuf.at[0], gbuf.at[of_x], g_s.at[i], g_r.at[i], (partner, z)).wait_recv()
            remote(fbuf.at[0], gbuf.at[4 + of_y], g_s.at[4 + i], g_r.at[4 + i], (partner, z)).wait_recv()

        lane = iota((ROWS, 128), 1)
        line, step = lane // 16, (lane // 4) % 4
        owner = jnp.where(line < 4, (line * 4 + step) * 2, (step * 4 + line - 4) * 2 + 1)
        mine = (place.astype(jnp.int32) == owner * 4 + lane % 4).astype(F32).astype(BF16)
        dterm[...] = dot_nn(mine, gbuf[...].reshape(128, CPAD))[:, 0:COLS]

    adapters = {"shrink": shrink, "reduce": reduce, "grow": grow, "sort": sort, "delta": deltas}
    for word in ORDER:
        if word in adapters:
            adapters[word]()
        elif word[0] == "r":
            greet(int(word[1]))
        elif word[0] == "w":
            weights(int(word[1]))
        elif word[0] == "m":
            multiply(int(word[1]), int(word[2]))
        elif word[0] == "s":
            stage(int(word[1]), int(word[2]))
        elif word[0] == "l":
            down(int(word[1]))
        else:
            gathered(int(word[0]), int(word[1]), word[2])

    for part in PARTS:
        if part != (0, 0, "F"):
            part_copy(*part).wait_send()
    for p in range(16):
        forward(p).wait_send()
    for n in range(CHUNKS):
        for s in range(8):
            long_hop(n, s, lbuf.at[n, s]).wait_send()
        for s in range(7):
            short_hop(n, s, sbuf.at[n, s]).wait_send()

    for q in range(4):

        @pl.when(4 * q + z_own != z)
        def _():
            remote(zsend.at[q], zrecv.at[z], z1_s.at[q], z1_r.at[z], (partner, z)).wait_send()

    @pl.when(lax.rem(z, 4) == z_own)
    def _():
        @pl.loop(1, NZ)
        def _(i):
            remote(zred, zgather.at[0], z2_s.at[i], z2_r.at[0], (partner, z)).wait_send()

    @pl.loop(1, 8)
    def _(i):
        remote(dbuf.at[i], ebuf.at[i], e_s.at[i], e_r.at[i], (partner, z)).wait_send()

    @pl.loop(1, 4)
    def _(i):
        remote(fbuf.at[0], gbuf.at[0], g_s.at[i], g_r.at[i], (partner, z)).wait_send()
        remote(fbuf.at[0], gbuf.at[0], g_s.at[4 + i], g_r.at[4 + i], (partner, z)).wait_send()

    for n in range(CHUNKS):
        for q in range(4):
            for c in range(2):
                others(n, q, c, lambda *a: result(*a).wait_send())
    for n in range(CHUNKS):
        for q in range(4):
            for c in range(2):
                others(n, q, c, lambda *a: result_arrives(*a).wait_recv())

    for k in range(NDP):
        got = rbuf[k].astype(F32)
        stack[k * SHARE : k * SHARE + 32] = jnp.where(left, got, 0.0)
        stack[k * SHARE + 32 : (k + 1) * SHARE] = jnp.where(left, 0.0, got)[0 : SHARE - 32]
    turn = jnp.where(iota((ROWS, 128), 1) % 64 == iota((ROWS, 128), 0), 1.0, 0.0).astype(BF16)
    v = dot_nt(turn, stack[...].astype(BF16)) + dterm[...]
    out_ref[...] = (0.5 * v * (1.0 + erf(v * 0.7071067811865476))).astype(BF16)


def local(tokens, base_up_matrix, adapter_down_maps, adapter_up_maps, request_adapter, adapter_storage):
    dma = pltpu.SemaphoreType.DMA
    vmem = pl.BlockSpec(memory_space=pltpu.VMEM)
    hbm = pl.BlockSpec(memory_space=pl.ANY)
    return pl.pallas_call(
        kernel,
        out_shape=jax.ShapeDtypeStruct((ROWS, COLS), BF16),
        in_specs=[vmem, hbm, hbm, hbm, vmem, vmem],
        out_specs=vmem,
        scratch_shapes=[
            pltpu.VMEM((WIDTH, WIDTH), BF16),
            pltpu.VMEM((128, WIDTH), BF16),
            pltpu.VMEM((128, COLS), BF16),
            pltpu.VMEM((16, 2, ROWS, WPAD), BF16),
            pltpu.VMEM((4, 256, WPAD), BF16),
            pltpu.VMEM((128, WPAD), BF16),
            pltpu.VMEM((CHUNKS, 8, CROWS, 128), F32),
            pltpu.VMEM((CHUNKS, 8, CROWS, 128), F32),
            pltpu.VMEM((CHUNKS, 2, CROWS, 128), BF16),
            pltpu.VMEM((16, 128, 128), BF16),
            pltpu.VMEM((CHUNKS, 8, CROWS, 128), BF16),
            pltpu.VMEM((CHUNKS, 7, CROWS, 128), BF16),
            pltpu.VMEM((CROWS, 128), F32),
            pltpu.VMEM((CHUNKS, 4, 2, 32, 128), BF16),
            pltpu.VMEM((NDP, 32, 128), BF16),
            pltpu.VMEM((COLS, 128), F32),
            pltpu.VMEM((16, 128, 128), BF16),
            pltpu.VMEM((4, 16, 128), BF16),
            pltpu.VMEM((NZ, 16, 128), BF16),
            pltpu.VMEM((16, 128), BF16),
            pltpu.VMEM((4, 16, 128), BF16),
            pltpu.VMEM((128, 128), F32),
            pltpu.VMEM((8, 16, CPAD), BF16),
            pltpu.VMEM((8, 16, CPAD), BF16),
            pltpu.VMEM((8, 16, CPAD), BF16),
            pltpu.VMEM((8, 16, CPAD), BF16),
            pltpu.VMEM((ROWS, COLS), F32),
            dma((3,)), dma((len(PARTS),)), dma((len(PARTS),)), dma((16,)), dma((16,)),
            dma((CHUNKS, 8)), dma((CHUNKS, 8)), dma((CHUNKS, 7)), dma((CHUNKS, 7)),
            dma((CHUNKS, 4, 2)), dma((CHUNKS, 4, 2)),
            dma((4,)), dma((NZ,)), dma((NZ,)), dma((4,)),
            dma((8,)), dma((8,)), dma((8,)), dma((8,)),
            pltpu.SemaphoreType.REGULAR((2,)),
        ],
        compiler_params=pltpu.CompilerParams(
            collective_id=0, has_side_effects=True, vmem_limit_bytes=56 * 1024 * 1024
        ),
        name="gather_sum_exchange",
    )(
        tokens,
        base_up_matrix.reshape(WIDTH, WIDTH),
        adapter_down_maps.reshape(128, WIDTH),
        adapter_up_maps.reshape(128, COLS),
        request_adapter.reshape(1, ROWS),
        adapter_storage.reshape(1, 64),
    )


def solution(mesh):
    return jax.shard_map(
        local,
        mesh=mesh,
        in_specs=(
            P("dp", "tensor"),
            P("tensor", "dp", None),
            P("dp", None, "tensor"),
            P("dp", None, "tensor"),
            P("dp", None),
            P(),
        ),
        out_specs=P("dp", "tensor"),
        check_vma=False,
    )
```

```python
import jax
import jax.numpy as jnp
from jax import lax
from jax.experimental import pallas as pl
from jax.experimental.pallas import tpu as pltpu
from jax.sharding import PartitionSpec as P

MESH = pl.DeviceIdType.MESH
F32 = jnp.float32
BF16 = jnp.bfloat16

NZ = 16
NDP = 32
ROWS = 64
WIDTH = 928
WPAD = 1024
SHARE = 58
SPAD = 64
CHUNKS = 4
CTOK = 512
CROWS = 240
COLS = 1856
CPAD = 1920

OFFSETS = (
    ((0, 0), (1, 0), (3, 0), (0, 1)),
    ((0, 3), (1, 1), (1, 3), (3, 1)),
    ((3, 3), (2, 0), (0, 2), (2, 1)),
    ((2, 3), (1, 2), (3, 2), (2, 2)),
)
POS = {offset: 4 * n + q for n, chunk in enumerate(OFFSETS) for q, offset in enumerate(chunk)}

PARTS = tuple(
    [(1, 0, "F"), (3, 0, "F"), (2, 0, "a"), (2, 0, "b")]
    + [(f, g, part) for f in range(4) for g, part in ((1, "F"), (3, "F"), (2, "a"), (2, "b"))]
)

ORDER = (
    "w0", "w1", "w2", "w3", "10F", "30F", "01F", "03F", "20a", "m00",
    "13F", "r1", "s00", "11F", "20b", "m01", "m02", "m03", "r2", "31F",
    "33F", "02a", "02b", "l0", "s01", "r3", "12b", "12a", "m10", "s10",
    "m11", "21F", "r4", "23F", "m12", "32a", "32b", "m13", "s02", "m20",
    "r5", "s20", "22a", "22b", "s11", "m21", "m22", "r6", "m23", "m30",
    "s30", "s03", "m31", "m32", "r7", "s21", "m33", "l1", "s12", "l2",
    "l3", "r8", "shrink", "s31", "s22", "s13", "s32", "s23", "s14", "reduce",
    "s33", "s24", "s04", "s34", "s25", "s15", "grow", "s35", "s05", "s26",
    "s36", "s16", "s06", "sort", "s37", "s27", "s17", "s07", "s38", "s28",
    "s18", "s08", "delta",
)


def dot_nt(a, b):
    return lax.dot_general(a, b, (((1,), (1,)), ((), ())), preferred_element_type=F32)


def dot_nn(a, b):
    return lax.dot_general(a, b, (((1,), (0,)), ((), ())), preferred_element_type=F32)


def iota(shape, dim):
    return lax.broadcasted_iota(jnp.int32, shape, dim)


def erf(x):
    x = jnp.clip(x, -4.0, 4.0)
    s = x * x
    p = -2.72614225801306e-10
    for c in (
        2.77068142495902e-08,
        -2.10102402082508e-06,
        -5.69250639462346e-05,
        -7.34990630326855e-04,
        -2.95459980854025e-03,
        -1.60960333262415e-02,
    ):
        p = p * s + c
    q = -1.45660718464996e-05
    for c in (-2.13374055278905e-04, -1.68282697438203e-03, -7.37332916720468e-03, -1.42647390514189e-02):
        q = q * s + c
    return x * p / q


def kernel(
    tok_ref, w_any, down_any, up_any, req_ref, sto_ref, out_ref,
    w_ref, down_ref, up_ref, xbuf, wt, low, ylong, yshort, first, h, lbuf, sbuf, both, total, rbuf, stack, sel,
    zsend, zrecv, zred, zgather, shrx, dbuf, ebuf, fbuf, gbuf, dterm,
    in_s, ag_s, ag_r, fw_s, fw_r, l_s, l_r, s_s, s_r, r_s, r_r,
    z1_s, z1_r, z2_s, z2_r, e_s, e_r, g_s, g_r, ring,
):
    dp = lax.axis_index("dp")
    z = lax.axis_index("tensor")
    core = lax.rem(dp, 2)
    cy = lax.rem(dp // 2, 4)
    cx = dp // 8
    along_own = cy + core * (cx - cy)
    first_core = along_own * 2 + core
    e_slot = core * 4 + along_own
    z_own = lax.rem(cx + cy + 2 * core, 4)
    way = 1 - 2 * core

    def dev(x, yy, c):
        return (lax.rem(x, 4) * 4 + lax.rem(yy, 4)) * 2 + c

    partner = dev(cx, cy, 1 - core)

    def along_first(other):
        spot, c = other // 2, lax.rem(other, 2)
        return dev(cx + core * (spot + 4 - cx), spot + core * (cy + 4 - spot), c)

    steps = {
        ("f", 1): dev(cx + core, cy + 1 - core, core),
        ("f", 3): dev(cx + 3 * core, cy + 3 * (1 - core), core),
        ("g", 1): dev(cx + 1 - core, cy + core, core),
        ("g", 3): dev(cx + 3 * (1 - core), cy + 3 * core, core),
    }

    def remote(src, dst, ssem, rsem, target):
        return pltpu.make_async_remote_copy(
            src_ref=src, dst_ref=dst, send_sem=ssem, recv_sem=rsem, device_id=target, device_id_type=MESH
        )

    barrier = pltpu.get_barrier_semaphore()
    above, below = (dp, lax.rem(z + 1, NZ)), (dp, lax.rem(z + NZ - 1, NZ))
    near = [(dev(cx + 1, cy, core), z), (dev(cx + 3, cy, core), z), (dev(cx, cy + 1, core), z)]
    near += [(dev(cx, cy + 3, core), z), (partner, z), above, below]
    for device in near:
        pl.semaphore_signal(barrier, inc=1, device_id=device, device_id_type=MESH)

    loads = {
        "w": pltpu.make_async_copy(w_any, w_ref, in_s.at[0]),
        "down": pltpu.make_async_copy(down_any, down_ref, in_s.at[1]),
        "up": pltpu.make_async_copy(up_any, up_ref, in_s.at[2]),
    }
    for load in loads.values():
        load.start()

    diagonal = iota((ROWS, ROWS), 0) == iota((ROWS, ROWS), 1)
    adapter = jnp.sum(jnp.where(diagonal, req_ref[...], 0), axis=1, keepdims=True)
    onehot = adapter == iota((ROWS, 64), 1)
    slot = jnp.sum(jnp.where(onehot, sto_ref[...], 0), axis=1, keepdims=True)
    lower = (iota((ROWS, ROWS), 1) < iota((ROWS, ROWS), 0)).astype(F32).astype(BF16)
    before = dot_nn(lower, onehot.astype(F32).astype(BF16))
    rank = jnp.sum(jnp.where(onehot, before, 0.0), axis=1, keepdims=True)
    place = slot.astype(F32) * 2.0 + rank
    xbuf[0, core, :, WPAD - 128 : WPAD] = jnp.broadcast_to(place, (ROWS, 128)).astype(BF16)
    xbuf[0, core, :, 0:WIDTH] = tok_ref[...]

    pl.semaphore_wait(barrier, len(near))

    def greet(k):
        if k > 0:
            pl.semaphore_wait(ring.at[0], 1)
            pl.semaphore_wait(ring.at[1], 1)
        if k < 8:
            pl.semaphore_signal(ring.at[0], inc=1, device_id=above, device_id_type=MESH)
            pl.semaphore_signal(ring.at[1], inc=1, device_id=below, device_id_type=MESH)

    greet(0)

    def where_at(f, g):
        return POS[g, f] + core * (POS[f, g] - POS[g, f])

    def part_copy(f, g, part):
        axis, d = ("f", f) if g == 0 else ("g", g)
        if part == "F":
            start, size, back, way_on = 0, ROWS, d, d
        else:
            start, size = (0, ROWS // 2) if part == "a" else (ROWS // 2, ROWS // 2)
            back = way_on = 1 if part == "a" else 3
        if part == "F":
            source = (0, 0) if g == 0 else (f, 0)
        else:
            source = (back, 0) if g == 0 else (f, back)
        i = PARTS.index((f, g, part))
        rows = pl.ds(start, size)
        return remote(
            xbuf.at[where_at(*source), core, rows], xbuf.at[where_at(f, g), core, rows],
            ag_s.at[i], ag_r.at[i], (steps[axis, way_on], z),
        )

    def forward(p):
        return remote(xbuf.at[p, core], xbuf.at[p, core], fw_s.at[p], fw_r.at[p], (partner, z))

    for part in ((1, 0, "F"), (3, 0, "F"), (0, 1, "F"), (0, 3, "F")):
        part_copy(*part).start()
    forward(0).start()

    low[...] = jnp.zeros_like(low)
    dbuf[...] = jnp.zeros_like(dbuf)
    ylong[:, :, CROWS - 8 : CROWS] = jnp.zeros((CHUNKS, 8, 8, 128), F32)
    yshort[:, :, CROWS - 8 : CROWS] = jnp.zeros((CHUNKS, 8, 8, 128), F32)

    arrived = {}

    def gathered(f, g, part):
        part_copy(f, g, part).wait_recv()
        if part == "F":
            half = "a" if (f if g == 0 else g) == 1 else "b"
            part_copy(2, 0, half).start() if g == 0 else part_copy(f, 2, half).start()
        else:
            arrived[f, g] = arrived.get((f, g), 0) + 1
            if arrived[f, g] < 2:
                return
        forward(where_at(f, g)).start()
        if g == 0:
            part_copy(f, 1, "F").start()
            part_copy(f, 3, "F").start()

    def offsets(b):
        return (8 - 2 * b, 9 + 2 * b, 7 - 2 * b, 10 + 2 * b)

    def weights(b):
        if b == 0:
            loads["w"].wait()
        row = iota((256, WIDTH), 0)
        plane = jnp.zeros((256, WIDTH), jnp.int32)
        for j, o in enumerate(offsets(b)):
            plane = jnp.where(row // SPAD == j, lax.rem(z + way * o + NZ, NZ), plane)
        unit = plane * SHARE + row % SPAD
        pickrow = jnp.where((row % SPAD < SHARE) & (unit == iota((256, WIDTH), 1)), 1.0, 0.0).astype(BF16)
        wt[b, :, WPAD - 128 : WPAD] = jnp.zeros((256, 128), BF16)
        wt[b, :, 0:WIDTH] = dot_nt(pickrow, w_ref[...]).astype(BF16)
        if b == 3:
            loads["down"].wait()
            low[:, 0:WIDTH] = down_ref[...]

    def multiply(n, b):
        if b == 0:
            for q in range(4):
                p = 4 * n + q
                remote(xbuf.at[p, 1 - core], xbuf.at[p, 1 - core], fw_s.at[p], fw_r.at[p], (partner, z)).wait_recv()
        x = xbuf[4 * n : 4 * n + 4].reshape(CTOK, WPAD)
        part = dot_nt(wt[b], x)
        for j in range(4):
            dest, s = (ylong, yshort)[j % 2], 2 * b + j // 2
            for q in range(4):
                dest[n, s, q * SHARE : (q + 1) * SHARE] = part[j * SPAD : j * SPAD + SHARE, q * 128 : (q + 1) * 128]

    def down(n):
        x = xbuf[4 * n : 4 * n + 4].reshape(CTOK, WPAD)
        part = dot_nt(low[...], x).astype(BF16)
        for q in range(4):
            h[4 * n + q] = part[:, q * 128 : (q + 1) * 128]

    def long_hop(n, s, src):
        return remote(src, lbuf.at[n, s], l_s.at[n, s], l_r.at[n, s], (dp, lax.rem(z + way + NZ, NZ)))

    def short_hop(n, s, src):
        return remote(src, sbuf.at[n, s], s_s.at[n, s], s_r.at[n, s], (dp, lax.rem(z - way + NZ, NZ)))

    def result(n, q, c):
        dx, dy = OFFSETS[n][q]
        target = dev(cx + 4 - dx, cy + 4 - dy, c)
        return remote(total.at[n, q, c], rbuf.at[dp], r_s.at[n, q, c], r_r.at[n, q, core], (target, z))

    def result_arrives(n, q, c):
        dx, dy = OFFSETS[n][q]
        source = dev(cx + dx, cy + dy, c)
        return remote(total.at[n, q, c], rbuf.at[source], r_s.at[n, q, c], r_r.at[n, q, c], (partner, z))

    def others(n, q, c, what):
        if n == 0 and q == 0:

            @pl.when(core != c)
            def _():
                what(n, q, c)

        else:
            what(n, q, c)

    left = iota((32, 128), 1) < 64

    def stage(n, s):
        if s == 0:
            first[n, 0] = ylong[n, 0].astype(BF16)
            long_hop(n, 0, first.at[n, 0]).start()
            first[n, 1] = yshort[n, 0].astype(BF16)
            short_hop(n, 0, first.at[n, 1]).start()
        if 1 <= s <= 7:
            here = lbuf.at[n, s - 1]
            long_hop(n, s - 1, here).wait_recv()
            lbuf[n, s - 1] = (lbuf[n, s - 1].astype(F32) + ylong[n, s]).astype(BF16)
            long_hop(n, s, here).start()
        if 1 <= s <= 6:
            here = sbuf.at[n, s - 1]
            short_hop(n, s - 1, here).wait_recv()
            sbuf[n, s - 1] = (sbuf[n, s - 1].astype(F32) + yshort[n, s]).astype(BF16)
            short_hop(n, s, here).start()
        if s == 8:
            short_hop(n, 6, sbuf.at[n, 6]).wait_recv()
            long_hop(n, 7, lbuf.at[n, 7]).wait_recv()
            both[...] = lbuf[n, 7].astype(F32) + sbuf[n, 6].astype(F32) + yshort[n, 7]
            for q in range(4):
                upper = both[q * SHARE : q * SHARE + 32]
                under = both[q * SHARE + 32 : q * SHARE + 64]
                total[n, q, 0] = jnp.where(left, upper, pltpu.roll(under, 64, 1)).astype(BF16)
                total[n, q, 1] = jnp.where(left, pltpu.roll(upper, 64, 1), under).astype(BF16)
                for c in range(2):
                    others(n, q, c, lambda *a: result(*a).start())
            if n == 0:
                rbuf[dp] = total[0, 0, core]

    lane64 = iota((64, 128), 1)

    def shrink():
        key = dp * 4
        for n in range(CHUNKS):
            for q in range(4):
                p = 4 * n + q
                dx, dy = OFFSETS[n][q]
                x = lax.rem(cx + 4 - dx, 4)
                yy = lax.rem(cy + 4 - dy, 4)
                along, across = yy + core * (x - yy), x + core * (yy - x)
                meta = dot_nt(
                    jnp.where(iota((16, 128), 1) == 127, 1.0, 0.0).astype(BF16),
                    xbuf[p, :, :, WPAD - 128 : WPAD].reshape(128, 128),
                )[0:1]
                row = iota((128, 128), 0)
                home = (along * 2 + iota((128, 128), 1) // 64) * 4 + across
                wanted = key + 2 * (row // 64) + row % 2
                hit = ((row % 64) // 2 == home) & (meta.astype(jnp.int32) == wanted)
                sel[p] = jnp.where(hit, 1.0, 0.0).astype(BF16)
        acc = jnp.zeros((128, 128), F32)
        for p in range(16):
            acc = acc + dot_nt(sel[p], h[p])
        part = jnp.where(lane64 < 64, acc[0:64], acc[64:128]).astype(BF16)
        for q in range(4):
            zsend[q] = part[16 * q : 16 * q + 16]
            owner = 4 * q + z_own

            @pl.when(owner != z)
            def _():
                remote(zsend.at[q], zrecv.at[z], z1_s.at[q], z1_r.at[z], (dp, owner)).start()

            @pl.when(owner == z)
            def _():
                zrecv[z] = zsend[q]

    def reduce():
        @pl.when(lax.rem(z, 4) == z_own)
        def _():
            @pl.loop(1, NZ)
            def _(i):
                other = lax.rem(z + i, NZ)
                remote(zsend.at[0], zrecv.at[other], z1_s.at[0], z1_r.at[other], (dp, other)).wait_recv()

            whole = zrecv[0].astype(F32)
            for i in range(1, NZ):
                whole = whole + zrecv[i].astype(F32)
            zred[...] = whole.astype(BF16)

            @pl.loop(1, NZ)
            def _(i):
                other = lax.rem(z + i, NZ)
                remote(zred, zgather.at[z // 4], z2_s.at[i], z2_r.at[z // 4], (dp, other)).start()

            zgather[z // 4] = zred[...]

    def grow():
        for q in range(4):

            @pl.when(4 * q + z_own != z)
            def _():
                remote(zred, zgather.at[q], z2_s.at[1], z2_r.at[q], (dp, 4 * q + z_own)).wait_recv()

        rows = zgather[...].reshape(64, 128).astype(F32)
        for g in range(8):
            eight = rows[8 * g : 8 * g + 8]
            lane = lane64[0:8]
            shrx[16 * g : 16 * g + 8] = jnp.where(lane < 64, eight, 0.0)
            shrx[16 * g + 8 : 16 * g + 16] = jnp.where(lane < 64, 0.0, eight)
        loads["up"].wait()
        grown = dot_nn(shrx[...].astype(BF16), up_ref[...])
        dbuf[:, :, 0:COLS] = grown.reshape(8, 16, COLS).astype(BF16)

        @pl.loop(1, 8)
        def _(i):
            other = lax.rem(first_core + i, 8)
            remote(dbuf.at[other], ebuf.at[e_slot], e_s.at[i], e_r.at[e_slot], (along_first(other), z)).start()

        ebuf[e_slot] = dbuf[first_core]

    def sort():
        @pl.loop(1, 8)
        def _(i):
            slot = lax.rem(e_slot + i, 8)
            remote(dbuf.at[slot], ebuf.at[slot], e_s.at[i], e_r.at[slot], (partner, z)).wait_recv()

        to = iota((128, 128), 0)
        place_of = to // 16
        origin = (place_of // 4) * 4 + (to // 4) % 4
        source = origin * 16 + ((to // 2) % 2) * 8 + (place_of % 4) * 2 + to % 2
        perm = jnp.where(iota((128, 128), 1) == source, 1.0, 0.0).astype(BF16)
        fbuf[...] = dot_nn(perm, ebuf[...].reshape(128, CPAD)).reshape(8, 16, CPAD).astype(BF16)

        @pl.loop(1, 4)
        def _(i):
            to_x, to_y = lax.rem(cx + i, 4), lax.rem(cy + i, 4)
            remote(fbuf.at[to_x], gbuf.at[cx], g_s.at[i], g_r.at[i], (dev(to_x, cy, core), z)).start()
            remote(fbuf.at[4 + to_y], gbuf.at[4 + cy], g_s.at[4 + i], g_r.at[4 + i], (dev(cx, to_y, core), z)).start()

        gbuf[cx] = fbuf[cx]
        gbuf[4 + cy] = fbuf[4 + cy]

    def deltas():
        @pl.loop(1, 4)
        def _(i):
            of_x, of_y = lax.rem(cx + 4 - i, 4), lax.rem(cy + 4 - i, 4)
            remote(fbuf.at[0], gbuf.at[of_x], g_s.at[i], g_r.at[i], (partner, z)).wait_recv()
            remote(fbuf.at[0], gbuf.at[4 + of_y], g_s.at[4 + i], g_r.at[4 + i], (partner, z)).wait_recv()

        lane = iota((ROWS, 128), 1)
        line, step = lane // 16, (lane // 4) % 4
        owner = jnp.where(line < 4, (line * 4 + step) * 2, (step * 4 + line - 4) * 2 + 1)
        mine = (place.astype(jnp.int32) == owner * 4 + lane % 4).astype(F32).astype(BF16)
        dterm[...] = dot_nn(mine, gbuf[...].reshape(128, CPAD))[:, 0:COLS]

    adapters = {"shrink": shrink, "reduce": reduce, "grow": grow, "sort": sort, "delta": deltas}
    for word in ORDER:
        if word in adapters:
            adapters[word]()
        elif word[0] == "r":
            greet(int(word[1]))
        elif word[0] == "w":
            weights(int(word[1]))
        elif word[0] == "m":
            multiply(int(word[1]), int(word[2]))
        elif word[0] == "s":
            stage(int(word[1]), int(word[2]))
        elif word[0] == "l":
            down(int(word[1]))
        else:
            gathered(int(word[0]), int(word[1]), word[2])

    for part in PARTS:
        if part != (0, 0, "F"):
            part_copy(*part).wait_send()
    for p in range(16):
        forward(p).wait_send()
    for n in range(CHUNKS):
        for s in range(8):
            long_hop(n, s, lbuf.at[n, s]).wait_send()
        for s in range(7):
            short_hop(n, s, sbuf.at[n, s]).wait_send()

    for q in range(4):

        @pl.when(4 * q + z_own != z)
        def _():
            remote(zsend.at[q], zrecv.at[z], z1_s.at[q], z1_r.at[z], (partner, z)).wait_send()

    @pl.when(lax.rem(z, 4) == z_own)
    def _():
        @pl.loop(1, NZ)
        def _(i):
            remote(zred, zgather.at[0], z2_s.at[i], z2_r.at[0], (partner, z)).wait_send()

    @pl.loop(1, 8)
    def _(i):
        remote(dbuf.at[i], ebuf.at[i], e_s.at[i], e_r.at[i], (partner, z)).wait_send()

    @pl.loop(1, 4)
    def _(i):
        remote(fbuf.at[0], gbuf.at[0], g_s.at[i], g_r.at[i], (partner, z)).wait_send()
        remote(fbuf.at[0], gbuf.at[0], g_s.at[4 + i], g_r.at[4 + i], (partner, z)).wait_send()

    for n in range(CHUNKS):
        for q in range(4):
            for c in range(2):
                others(n, q, c, lambda *a: result(*a).wait_send())
    for n in range(CHUNKS):
        for q in range(4):
            for c in range(2):
                others(n, q, c, lambda *a: result_arrives(*a).wait_recv())

    for k in range(NDP):
        got = rbuf[k].astype(F32)
        stack[k * SHARE : k * SHARE + 32] = jnp.where(left, got, 0.0)
        stack[k * SHARE + 32 : (k + 1) * SHARE] = jnp.where(left, 0.0, got)[0 : SHARE - 32]
    turn = jnp.where(iota((ROWS, 128), 1) % 64 == iota((ROWS, 128), 0), 1.0, 0.0).astype(BF16)
    v = dot_nt(turn, stack[...].astype(BF16)) + dterm[...]
    out_ref[...] = (0.5 * v * (1.0 + erf(v * 0.7071067811865476))).astype(BF16)


def local(tokens, base_up_matrix, adapter_down_maps, adapter_up_maps, request_adapter, adapter_storage):
    dma = pltpu.SemaphoreType.DMA
    vmem = pl.BlockSpec(memory_space=pltpu.VMEM)
    hbm = pl.BlockSpec(memory_space=pl.ANY)
    return pl.pallas_call(
        kernel,
        out_shape=jax.ShapeDtypeStruct((ROWS, COLS), BF16),
        in_specs=[vmem, hbm, hbm, hbm, vmem, vmem],
        out_specs=vmem,
        scratch_shapes=[
            pltpu.VMEM((WIDTH, WIDTH), BF16),
            pltpu.VMEM((128, WIDTH), BF16),
            pltpu.VMEM((128, COLS), BF16),
            pltpu.VMEM((16, 2, ROWS, WPAD), BF16),
            pltpu.VMEM((4, 256, WPAD), BF16),
            pltpu.VMEM((128, WPAD), BF16),
            pltpu.VMEM((CHUNKS, 8, CROWS, 128), F32),
            pltpu.VMEM((CHUNKS, 8, CROWS, 128), F32),
            pltpu.VMEM((CHUNKS, 2, CROWS, 128), BF16),
            pltpu.VMEM((16, 128, 128), BF16),
            pltpu.VMEM((CHUNKS, 8, CROWS, 128), BF16),
            pltpu.VMEM((CHUNKS, 7, CROWS, 128), BF16),
            pltpu.VMEM((CROWS, 128), F32),
            pltpu.VMEM((CHUNKS, 4, 2, 32, 128), BF16),
            pltpu.VMEM((NDP, 32, 128), BF16),
            pltpu.VMEM((COLS, 128), F32),
            pltpu.VMEM((16, 128, 128), BF16),
            pltpu.VMEM((4, 16, 128), BF16),
            pltpu.VMEM((NZ, 16, 128), BF16),
            pltpu.VMEM((16, 128), BF16),
            pltpu.VMEM((4, 16, 128), BF16),
            pltpu.VMEM((128, 128), F32),
            pltpu.VMEM((8, 16, CPAD), BF16),
            pltpu.VMEM((8, 16, CPAD), BF16),
            pltpu.VMEM((8, 16, CPAD), BF16),
            pltpu.VMEM((8, 16, CPAD), BF16),
            pltpu.VMEM((ROWS, COLS), F32),
            dma((3,)), dma((len(PARTS),)), dma((len(PARTS),)), dma((16,)), dma((16,)),
            dma((CHUNKS, 8)), dma((CHUNKS, 8)), dma((CHUNKS, 7)), dma((CHUNKS, 7)),
            dma((CHUNKS, 4, 2)), dma((CHUNKS, 4, 2)),
            dma((4,)), dma((NZ,)), dma((NZ,)), dma((4,)),
            dma((8,)), dma((8,)), dma((8,)), dma((8,)),
            pltpu.SemaphoreType.REGULAR((2,)),
        ],
        compiler_params=pltpu.CompilerParams(
            collective_id=0, has_side_effects=True, vmem_limit_bytes=56 * 1024 * 1024
        ),
        name="gather_sum_exchange",
    )(
        tokens,
        base_up_matrix.reshape(WIDTH, WIDTH),
        adapter_down_maps.reshape(128, WIDTH),
        adapter_up_maps.reshape(128, COLS),
        request_adapter.reshape(1, ROWS),
        adapter_storage.reshape(1, 64),
    )


def solution(mesh):
    return jax.shard_map(
        local,
        mesh=mesh,
        in_specs=(
            P("dp", "tensor"),
            P("tensor", "dp", None),
            P("dp", None, "tensor"),
            P("dp", None, "tensor"),
            P("dp", None),
            P(),
        ),
        out_specs=P("dp", "tensor"),
        check_vma=False,
    )
```
